1024 devices in a mesh: rx: 4 (over x_hi, core), space: 256 (over x_lo, y, z).
Axes of the slice: x: 4 (x_hi: 2, x_lo: 2; x = x_hi * 2 + x_lo), y: 8, z: 16, core: 2. Of those that a mesh axis runs over, the one named last changes fastest.
Arguments:
- conductivity: float32 [768, 32, 128], P('space'), may hold values from 0.1 to 1
- background: float32 [4, 2, 3, 768, 32, 128], P(None, None, None, 'space'), may hold values from -6 to 6
- warm_start: float32 [8, 2, 3, 768, 32, 128], P('rx', None, None, 'space'), may hold values from -8 to 8
- data_weight: float32 [8, 2, 3], P('rx'), may hold values from -2560 to 2560
- recv_cell: int32 [8], P('rx'), may hold values from 0 to 3145727
- src_group: int32 [8], P('rx'), may hold values from 0 to 3
- group_freq: int32 [4], replicated, may hold values from 0 to 7
Outputs:
- block: float32 [16, 16], P('rx')
- smoothed: bfloat16 [8, 2, 768, 32, 128], P('rx', None, 'space')
The draws below stay inside these ranges and needn't reach their ends.
All inputs are finite; a program needn't handle non-finite values.
Results may differ from the reference program's by a relative error of at most 0.01.
Values may be sent and summed in bfloat16 or wider, within the bound.
A program may use at most 32 MiB of HBM per device.

```python
import math
import jax
import jax.numpy as jnp
from jax import lax

NY = 32
NZ = 128
G = 4
NFREQ = 8
ITERS = 3
SOURCES = 8
NX = 768


def draw_warm_start(key, part):
    key_common, key_own = jax.random.split(jax.random.fold_in(key, 11))
    common_shape = (1, 2, 3, NX, NY, NZ)
    own_shape = (SOURCES, 2, 3, NX, NY, NZ)
    common = jax.random.normal(key_common, common_shape, jnp.float32)
    own = jax.random.normal(key_own, own_shape, jnp.float32)
    return jnp.clip(common + 0.7 * own, -8.0, 8.0)


def with_ends(values, rng, smallest, largest):
    extent = values.shape
    place = [jax.random.randint(jax.random.fold_in(rng, axis), (), 0, extent[axis]) for axis in range(len(extent))]
    values = values.at[tuple(place)].set(smallest)
    longest = extent.index(max(extent))
    place[longest] = (place[longest] + 1) % extent[longest]
    return values.at[tuple(place)].set(largest)


def block_scale(key, shape, cuts, smallest, high):
    gain, own = 1.0, jax.random.fold_in(key, 6)
    for position, shards_of in cuts:
        draws = jnp.exp(jax.random.uniform(jax.random.fold_in(own, position), (shards_of,), jnp.float32, smallest / len(cuts), high / len(cuts)))
        gain = gain * jnp.repeat(draws, shape[position] // shards_of).reshape([-1 if axis == position else 1 for axis in range(len(shape))])
    return gain


def noise(rng, dims, width, bound, cuts=(), held_as=jnp.bfloat16):
    drawn = jax.random.normal(rng, dims, jnp.float32) * width
    if len(cuts) > 0:
        drawn = block_scale(rng, dims, cuts, -0.22, 0.18) * drawn
    return jnp.clip(drawn, min=-bound, max=bound).astype(held_as)


def setup_inputs(seed: int = 0) -> dict:
    seeds = jax.random.split(jax.random.key(seed), 8)
    return {
        "conductivity": jnp.clip(jnp.exp(math.log(1.0) - 2.3025851 * jax.random.uniform(seeds[0], (NX, NY, NZ), jnp.float32) ** block_scale(seeds[0], (NX, NY, NZ), ((0, 256),), -0.2, 0.2)), 0.1, 1.0),
        "background": noise(seeds[1], (G, 2, 3, NX, NY, NZ), 1.0, 6.0, ((3, 256),), jnp.float32),
        "warm_start": draw_warm_start(jax.random.fold_in(seeds[7], 71), 0),
        "data_weight": noise(seeds[3], (SOURCES, 2, 3), ((NX * NY * NZ) ** 0.5 / 4), 2560.0, ((0, 4),), jnp.float32),
        "recv_cell": with_ends(jax.random.randint(seeds[4], (SOURCES,), 0, NX * NY * NZ), jax.random.fold_in(seeds[4], 1), 0, (NX * NY * NZ) - 1).astype(jnp.int32),
        "src_group": with_ends(jax.random.randint(seeds[5], (SOURCES,), 0, G), jax.random.fold_in(seeds[5], 1), 0, G - 1).astype(jnp.int32),
        "group_freq": with_ends(jax.random.randint(seeds[6], (G,), 0, NFREQ), jax.random.fold_in(seeds[6], 1), 0, NFREQ - 1).astype(jnp.int32),
    }


RELAX = 0.2
KAPPA = 0.1


def forward_y(f):
    return jnp.concatenate([f[..., 1:, :] - f[..., :-1, :], -f[..., -1:, :]], axis=-2)


def forward_z(f):
    return jnp.concatenate([f[..., 1:] - f[..., :-1], -f[..., -1:]], axis=-1)


def backward_y(f):
    return jnp.concatenate([f[..., :1, :], f[..., 1:, :] - f[..., :-1, :]], axis=-2)


def backward_z(f):
    return jnp.concatenate([f[..., :1], f[..., 1:] - f[..., :-1]], axis=-1)


def curl_curl(padded):
    comp_x = padded[..., 0, :, :, :]
    comp_y = padded[..., 1, :, :, :]
    comp_z = padded[..., 2, :, :, :]
    low_x = comp_x[..., :-1, :, :]
    low_y = comp_y[..., :-1, :, :]
    low_z = comp_z[..., :-1, :, :]
    mag_x = forward_y(low_z) - forward_z(low_y)
    mag_y = forward_z(low_x) - (comp_z[..., 1:, :, :] - comp_z[..., :-1, :, :])
    mag_z = (comp_y[..., 1:, :, :] - comp_y[..., :-1, :, :]) - forward_y(low_x)
    curl_x = backward_y(mag_z[..., 1:, :, :]) - backward_z(mag_y[..., 1:, :, :])
    curl_y = backward_z(mag_x[..., 1:, :, :]) - (mag_z[..., 1:, :, :] - mag_z[..., :-1, :, :])
    curl_z = (mag_y[..., 1:, :, :] - mag_y[..., :-1, :, :]) - backward_y(mag_x[..., 1:, :, :])
    return jnp.stack([curl_x, curl_y, curl_z], axis=-4)


def operate(adjoint, padded, coef):
    curl = curl_curl(padded)
    real_part = curl[..., 0, :, :, :, :] - coef * adjoint[..., 1, :, :, :, :]
    imag_part = curl[..., 1, :, :, :, :] + coef * adjoint[..., 0, :, :, :, :]
    return jnp.stack([real_part, imag_part], axis=-5)


def sensitivity(adjoint, field, coef):
    field_re = field[..., 0, :, :, :, :]
    field_im = field[..., 1, :, :, :, :]
    adj_re = adjoint[..., 0, :, :, :, :]
    adj_im = adjoint[..., 1, :, :, :, :]
    prod_re = jnp.sum(field_re * adj_re - field_im * adj_im, axis=-4)
    prod_im = jnp.sum(field_re * adj_im + field_im * adj_re, axis=-4)
    return (coef * jnp.stack([prod_re, prod_im], axis=-4)).astype(jnp.bfloat16)


def neighbours_y(f):
    zeros = jnp.zeros_like(f[..., :1, :])
    return jnp.concatenate([f[..., 1:, :], zeros], axis=-2) + jnp.concatenate([zeros, f[..., :-1, :]], axis=-2)


def neighbours_z(f):
    zeros = jnp.zeros_like(f[..., :1])
    return jnp.concatenate([f[..., 1:], zeros], axis=-1) + jnp.concatenate([zeros, f[..., :-1]], axis=-1)


def smooth_step(padded):
    centre = padded[..., 1:-1, :, :]
    near = padded[..., 2:, :, :] + padded[..., :-2, :, :] + neighbours_y(centre) + neighbours_z(centre)
    return centre + KAPPA * (near - 6.0 * centre)


def reference(conductivity, background, warm_start, data_weight, recv_cell, src_group, group_freq):
    cells = NX * NY * NZ
    flat = jnp.arange(cells, dtype=jnp.int32).reshape(NX, NY, NZ)

    def one_source(items):
        start, weight, cell, group = items
        field = background[group]
        angular = 0.25 * jnp.power(jnp.float32(1.25), group_freq[group].astype(jnp.float32))
        coef = angular * conductivity
        point = (flat == cell).astype(jnp.float32)
        source_term = weight[:, :, None, None, None] * point
        adjoint = start
        for sweep in range(ITERS):
            padded = jnp.pad(adjoint, ((0, 0), (0, 0), (1, 1), (0, 0), (0, 0)))
            adjoint = adjoint + RELAX * (source_term - operate(adjoint, padded, coef))
        return sensitivity(adjoint, field, coef)

    rows = lax.map(one_source, (warm_start, data_weight, recv_cell, src_group))

    def smooth_one(row):
        value = row.astype(jnp.float32)
        for sweep in range(2):
            value = smooth_step(jnp.pad(value, ((0, 0), (1, 1), (0, 0), (0, 0))))
        return value.astype(jnp.bfloat16)

    smoothed = lax.map(smooth_one, rows)
    flat_rows = rows.reshape(2 * SOURCES, cells)
    flat_smooth = smoothed.reshape(2 * SOURCES, cells)
    block = jnp.dot(flat_rows, flat_smooth.T, preferred_element_type=jnp.float32) / cells
    return block, smoothed
```

```python
import functools

import jax
import jax.numpy as jnp
from jax import lax
from jax.experimental import pallas as pl
from jax.experimental.pallas import tpu as pltpu
from jax.sharding import PartitionSpec as P

ITERS = 3
RELAX = 0.2
KAPPA = 0.1
MESH = pl.DeviceIdType.MESH


def kernel(
    peers,
    lines,
    rx_peers,
    cond_hbm,
    back_hbm,
    warm_hbm,
    weight_hbm,
    cell_hbm,
    group_hbm,
    freq_hbm,
    block_ref,
    smooth_hbm,
    cond,
    back,
    warm,
    weight,
    cell,
    group,
    freq,
    send,
    csend,
    land,
    cland,
    first,
    second,
    third,
    rows,
    rland,
    smooth,
    sums,
    line_sums,
    plane_sums,
    load_sem,
    out_sem,
    send_sem,
    recv_sem,
    rsend_sem,
    rrecv_sem,
    gsend_sem,
    grecv_sem,
    ssend_sem,
    srecv_sem,
):
    depth = cond.shape[0]
    height, breadth = cond.shape[1:]
    count = warm.shape[0]
    rx = lax.axis_index("rx")
    me = lax.axis_index("space")
    columns = peers // lines
    line = me // columns
    column = me % columns
    after = (rx, (me + 1) % peers)
    before = (rx, (me + peers - 1) % peers)
    others = [((rx + k) % rx_peers, me) for k in range(1, rx_peers)]
    along = [(rx, line * columns + (column + k) % columns) for k in range(1, columns)]
    across = [(rx, ((line + k) % lines) * columns + column) for k in range(1, lines)]

    loads = [
        pltpu.make_async_copy(src, dst, load_sem.at[i])
        for i, (src, dst) in enumerate(
            (
                (warm_hbm, warm),
                (cond_hbm, cond),
                (weight_hbm, weight),
                (cell_hbm, cell),
                (group_hbm, group),
                (freq_hbm, freq),
                (back_hbm, back),
            )
        )
    ]
    for load in loads:
        load.start()
    barrier = pltpu.get_barrier_semaphore()
    partners = [before, after] + others + along + across
    for partner in partners:
        pl.semaphore_signal(barrier, inc=1, device_id=partner, device_id_type=MESH)

    for load in loads[:2]:
        load.wait()
    csend[...] = cond[...].astype(jnp.bfloat16)

    def pack(s, carry):
        for p in range(2):
            for c in range(3):
                send[:, c, 2 * s + p] = warm[s, p, c].astype(jnp.bfloat16)
        return carry

    lax.fori_loop(0, count, pack, 0)
    pl.semaphore_wait(barrier, len(partners))

    copies = []
    for k in range(depth):
        for way, target in ((0, after), (1, before)):
            plane = depth - 1 - k if way == 0 else k
            copies.append(
                pltpu.make_async_remote_copy(
                    send.at[plane],
                    land.at[way, plane],
                    send_sem.at[way, k],
                    recv_sem.at[way, k],
                    device_id=target,
                    device_id_type=MESH,
                )
            )
    ccopies = [
        pltpu.make_async_remote_copy(
            csend,
            cland.at[way],
            send_sem.at[way, depth],
            recv_sem.at[way, depth],
            device_id=target,
            device_id_type=MESH,
        )
        for way, target in ((0, after), (1, before))
    ]
    for copy in copies[:2] + ccopies + copies[2:]:
        copy.start()

    for load in loads[2:]:
        load.wait()
    has_before = (me > 0).astype(jnp.float32)
    has_after = (me < peers - 1).astype(jnp.float32)
    iy = lax.broadcasted_iota(jnp.int32, (height, breadth), 0)
    iz = lax.broadcasted_iota(jnp.int32, (height, breadth), 1)
    flat = iy * breadth + iz

    def y_up(f):
        return jnp.where(iy == height - 1, 0.0, pltpu.roll(f, height - 1, 0))

    def y_down(f):
        return jnp.where(iy == 0, 0.0, pltpu.roll(f, 1, 0))

    def z_up(f):
        return jnp.where(iz == breadth - 1, 0.0, pltpu.roll(f, breadth - 1, 1))

    def z_down(f):
        return jnp.where(iz == 0, 0.0, pltpu.roll(f, 1, 1))

    def angular_of(s):
        k = freq[group[s]]
        low = jnp.where(k % 2 == 1, jnp.float32(1.25), jnp.float32(1.0))
        mid = jnp.where((k // 2) % 2 == 1, jnp.float32(1.25**2), jnp.float32(1.0))
        top = jnp.where((k // 4) % 2 == 1, jnp.float32(1.25**4), jnp.float32(1.0))
        return 0.25 * (low * mid * top)

    def guard(plane, f):
        if plane < depth:
            return f * has_before
        if plane >= 2 * depth:
            return f * has_after
        return f

    def start_plane(s, p, c, plane):
        if plane < depth:
            return guard(plane, land[0, plane, c, 2 * s + p].astype(jnp.float32))
        if plane >= 2 * depth:
            return guard(plane, land[1, plane - 2 * depth, c, 2 * s + p].astype(jnp.float32))
        return warm[s, p, c, plane - depth]

    def cond_plane(plane):
        if plane < depth:
            return cland[0, plane].astype(jnp.float32)
        if plane >= 2 * depth:
            return cland[1, plane - 2 * depth].astype(jnp.float32)
        return cond[plane - depth]

    def stored(buffer):
        return lambda s, p, c, plane: buffer[2 * s + p, c, plane]

    def sweep(source, target, low, high):
        def one(i, carry):
            s, p = i // 2, i % 2
            turn = (1 - 2 * p).astype(jnp.float32) * (RELAX * angular_of(s))
            old = {
                (c, plane): source(s, p, c, plane)
                for plane in range(low - 1, high + 1)
                for c in range(3)
            }

            def mag_y(plane):
                ex = old[0, plane]
                return (z_up(ex) - ex) - (old[2, plane + 1] - old[2, plane])

            def mag_z(plane):
                ex = old[0, plane]
                return (old[1, plane + 1] - old[1, plane]) - (y_up(ex) - ex)

            hy_low, hz_low = mag_y(low - 1), mag_z(low - 1)
            for plane in range(low, high):
                ey, ez = old[1, plane], old[2, plane]
                hx = (y_up(ez) - ez) - (z_up(ey) - ey)
                hy, hz = mag_y(plane), mag_z(plane)
                curl = (
                    (hz - y_down(hz)) - (hy - z_down(hy)),
                    (hx - z_down(hx)) - (hz - hz_low),
                    (hy - hy_low) - (hx - y_down(hx)),
                )
                hy_low, hz_low = hy, hz
                factor = turn * cond_plane(plane)
                here = cell[s] - (me * depth + plane - depth) * (height * breadth)
                point = flat == here
                for c in range(3):
                    other = source(s, 1 - p, c, plane)
                    term = jnp.where(point, RELAX * weight[s, p, c], 0.0)
                    new = old[c, plane] + term - RELAX * curl[c] + factor * other
                    target[i, c, plane] = guard(plane, new)
            return carry

        lax.fori_loop(0, 2 * count, one, 0)

    own = (depth, 2 * depth)
    for copy in copies + ccopies:
        copy.wait_recv()
    sweep(start_plane, first, own[0] - 2, own[1] + 2)
    sweep(stored(first), second, own[0] - 1, own[1] + 1)
    sweep(stored(second), third, own[0], own[1])

    def products(s, carry):
        g = group[s]
        angular = angular_of(s)
        for plane in range(depth):
            real = jnp.zeros((height, breadth), jnp.float32)
            imag = jnp.zeros((height, breadth), jnp.float32)
            for c in range(3):
                fr, fi = back[g, 0, c, plane], back[g, 1, c, plane]
                ar, ai = third[2 * s, c, depth + plane], third[2 * s + 1, c, depth + plane]
                real += fr * ar - fi * ai
                imag += fr * ai + fi * ar
            coef = angular * cond[plane]
            rows[rx, plane, 2 * s] = (coef * real).astype(jnp.bfloat16)
            rows[rx, plane, 2 * s + 1] = (coef * imag).astype(jnp.bfloat16)
        return carry

    lax.fori_loop(0, count, products, 0)

    halo = [
        pltpu.make_async_remote_copy(
            rows.at[rx, pl.ds(start, 2)],
            rland.at[way],
            rsend_sem.at[way],
            rrecv_sem.at[way],
            device_id=target,
            device_id_type=MESH,
        )
        for way, target, start in ((0, after, depth - 2), (1, before, 0))
    ]
    gather = [
        pltpu.make_async_remote_copy(
            rows.at[rx],
            rows.at[rx],
            gsend_sem.at[k],
            grecv_sem.at[k],
            device_id=target,
            device_id_type=MESH,
        )
        for k, target in enumerate(others)
    ]
    for copy in halo + gather:
        copy.start()
    for copy in halo:
        copy.wait_recv()

    def smoothing(r, carry):
        planes = (
            [rland[0, k, r].astype(jnp.float32) * has_before for k in range(2)]
            + [rows[rx, k, r].astype(jnp.float32) for k in range(depth)]
            + [rland[1, k, r].astype(jnp.float32) * has_after for k in range(2)]
        )
        for step in range(2):
            ends = [planes[0], planes[-1]]
            planes = [
                planes[k]
                + KAPPA
                * (
                    planes[k - 1]
                    + planes[k + 1]
                    + y_up(planes[k])
                    + y_down(planes[k])
                    + z_up(planes[k])
                    + z_down(planes[k])
                    - 6.0 * planes[k]
                )
                for k in range(1, len(planes) - 1)
            ]
            if step == 0:
                planes[0] = planes[0] * has_before
                planes[-1] = planes[-1] * has_after
        for k in range(depth):
            smooth[r, k] = planes[k].astype(jnp.bfloat16)
        return carry

    lax.fori_loop(0, 2 * count, smoothing, 0)
    out = pltpu.make_async_copy(smooth, smooth_hbm, out_sem)
    out.start()

    for copy in gather:
        copy.wait_recv()

    def dots(b, carry):
        peer, r = b // (2 * count), b % (2 * count)
        for a in range(2 * count):
            total = jnp.zeros((8, breadth), jnp.float32)
            for k in range(depth):
                product = smooth[a, k].astype(jnp.float32) * rows[peer, k, r].astype(jnp.float32)
                for j in range(height // 8):
                    total += product[8 * j : 8 * j + 8]
            sums[a, b] = jnp.sum(total, axis=0)
        return carry

    lax.fori_loop(0, 2 * count * rx_peers, dots, 0)
    ones = jnp.ones((8, breadth), jnp.float32)
    wide = 2 * count * rx_peers
    line_sums[column] = jnp.zeros(line_sums.shape[1:], jnp.float32)
    for a in range(2 * count):
        lanes = lax.dot_general(
            ones,
            sums[a],
            (((1,), (1,)), ((), ())),
            precision=lax.Precision.HIGHEST,
            preferred_element_type=jnp.float32,
        )
        line_sums[column, a : a + 1, 0:wide] = lanes[0:1]

    step_one = [
        pltpu.make_async_remote_copy(
            line_sums.at[column],
            line_sums.at[column],
            ssend_sem.at[0, k],
            srecv_sem.at[0, k],
            device_id=target,
            device_id_type=MESH,
        )
        for k, target in enumerate(along)
    ]
    for copy in step_one:
        copy.start()
    for copy in step_one:
        copy.wait_recv()
    plane_sums[line] = jnp.sum(line_sums[...], axis=0)
    step_two = [
        pltpu.make_async_remote_copy(
            plane_sums.at[line],
            plane_sums.at[line],
            ssend_sem.at[1, k],
            srecv_sem.at[1, k],
            device_id=target,
            device_id_type=MESH,
        )
        for k, target in enumerate(across)
    ]
    for copy in step_two:
        copy.start()
    for copy in step_two:
        copy.wait_recv()
    total = jnp.sum(plane_sums[...], axis=0)
    cells = depth * height * breadth * peers
    block_ref[...] = total[0 : 2 * count, 0:wide] / cells
    for copy in copies + ccopies + halo + gather + step_one + step_two:
        copy.wait_send()
    out.wait()


def shards(conductivity, background, warm_start, data_weight, recv_cell, src_group, group_freq):
    count = warm_start.shape[0]
    depth, height, breadth = conductivity.shape
    peers, rx_peers = lax.axis_size("space"), lax.axis_size("rx")
    lines = 1
    while lines * lines < peers:
        lines *= 2
    columns = peers // lines
    rows = 2 * count
    wide = rows * rx_peers
    plane = (height, breadth)
    f32, b16 = jnp.float32, jnp.bfloat16
    vmem, dma = pltpu.VMEM, pltpu.SemaphoreType.DMA
    hbm = pl.BlockSpec(memory_space=pltpu.HBM)
    block, smoothed = pl.pallas_call(
        functools.partial(kernel, peers, lines, rx_peers),
        name="inversion_step",
        out_shape=(
            jax.ShapeDtypeStruct((rows, wide), f32),
            jax.ShapeDtypeStruct((rows, depth) + plane, b16),
        ),
        in_specs=[hbm] * 7,
        out_specs=(pl.BlockSpec(memory_space=vmem), hbm),
        scratch_shapes=[
            vmem(conductivity.shape, f32),
            vmem(background.shape, f32),
            vmem(warm_start.shape, f32),
            pltpu.SMEM(data_weight.shape, f32),
            pltpu.SMEM(recv_cell.shape, jnp.int32),
            pltpu.SMEM(src_group.shape, jnp.int32),
            pltpu.SMEM(group_freq.shape, jnp.int32),
            vmem((depth, 3, rows) + plane, b16),
            vmem((depth,) + plane, b16),
            vmem((2, depth, 3, rows) + plane, b16),
            vmem((2, depth) + plane, b16),
            vmem((rows, 3, 3 * depth) + plane, f32),
            vmem((rows, 3, 3 * depth) + plane, f32),
            vmem((rows, 3, 3 * depth) + plane, f32),
            vmem((rx_peers, depth, rows) + plane, b16),
            vmem((2, 2, rows) + plane, b16),
            vmem((rows, depth) + plane, b16),
            vmem((rows, wide, breadth), f32),
            vmem((columns, 8, 128), f32),
            vmem((lines, 8, 128), f32),
            dma((7,)),
            dma,
            dma((2, depth + 1)),
            dma((2, depth + 1)),
            dma((2,)),
            dma((2,)),
            dma((rx_peers - 1,)),
            dma((rx_peers - 1,)),
            dma((2, max(lines, columns) - 1)),
            dma((2, max(lines, columns) - 1)),
        ],
        compiler_params=pltpu.CompilerParams(
            collective_id=0, has_side_effects=True, vmem_limit_bytes=48 * 2**20
        ),
    )(conductivity, background, warm_start, data_weight, recv_cell, src_group, group_freq)
    return block, smoothed.reshape((count, 2, depth) + plane)


def solution(mesh):
    in_specs = (
        P("space", None, None),
        P(None, None, None, "space", None, None),
        P("rx", None, None, "space", None, None),
        P("rx", None, None),
        P("rx"),
        P("rx"),
        P(),
    )
    out_specs = (P("rx", None), P("rx", None, "space", None, None))
    return jax.shard_map(shards, mesh=mesh, in_specs=in_specs, out_specs=out_specs, check_vma=False)
```

```python
import functools

import jax
import jax.numpy as jnp
from jax import lax
from jax.experimental import pallas as pl
from jax.experimental.pallas import tpu as pltpu
from jax.sharding import PartitionSpec as P

ITERS = 3
RELAX = 0.2
KAPPA = 0.1
MESH = pl.DeviceIdType.MESH


def kernel(
    peers,
    lines,
    rx_peers,
    cond_hbm,
    back_hbm,
    warm_hbm,
    weight_hbm,
    cell_hbm,
    group_hbm,
    freq_hbm,
    block_ref,
    smooth,
    cond,
    back,
    warm,
    weight,
    cell,
    group,
    freq,
    send,
    mix,
    csend,
    land,
    cland,
    first,
    second,
    third,
    rows,
    rland,
    sums,
    line_sums,
    plane_sums,
    load_sem,
    send_sem,
    recv_sem,
    rsend_sem,
    rrecv_sem,
    gsend_sem,
    grecv_sem,
    ssend_sem,
    srecv_sem,
    meet_sem,
):
    depth = cond.shape[0]
    height, breadth = cond.shape[1:]
    count = warm.shape[0]
    rx = lax.axis_index("rx")
    me = lax.axis_index("space")
    columns = peers // lines
    line = me // columns
    column = me % columns
    after = (rx, (me + 1) % peers)
    before = (rx, (me + peers - 1) % peers)
    others = [((rx + k) % rx_peers, me) for k in range(1, rx_peers)]

    def at(line, column):
        return (rx, (line % lines) * columns + column % columns)

    along = [at(line, column + k) for k in range(1, columns)]
    across = [at(line + k, column) for k in range(1, lines)]
    rows_y = lines // 2
    half = (line // rows_y) * rows_y

    def beside(k):
        return at(half + (line + k + rows_y) % rows_y, column)

    opposite = at(line + rows_y, column)

    loads = [
        pltpu.make_async_copy(src, dst, load_sem.at[i])
        for i, (src, dst) in enumerate(
            (
                (warm_hbm, warm),
                (cond_hbm, cond),
                (weight_hbm, weight),
                (cell_hbm, cell),
                (group_hbm, group),
                (freq_hbm, freq),
                (back_hbm, back),
            )
        )
    ]
    for load in loads:
        load.start()
    barrier = pltpu.get_barrier_semaphore()
    near = [at(line, column + 1), at(line, column - 1), opposite]
    if rows_y > 1:
        near += [beside(1), beside(-1)]
    partners = [before, after] + near + others
    for partner in partners:
        pl.semaphore_signal(barrier, inc=1, device_id=partner, device_id_type=MESH)

    meetings = []
    reach, y_steps = 1, 0
    while reach < max(columns, rows_y) // 2:
        targets = []
        if reach < columns // 2:
            targets += [at(line, column + reach), at(line, column - reach)]
        if reach < rows_y // 2:
            targets += [beside(reach), beside(-reach)]
            y_steps += 1
        meetings.append(targets)
        reach *= 2
    if len(meetings) == y_steps:
        meetings.append([])
    meetings[y_steps].append(opposite)
    taken = []

    def meet(steps):
        while len(taken) < min(steps, len(meetings) + 1):
            step = len(taken)
            if step > 0:
                pl.semaphore_wait(meet_sem.at[step - 1], len(meetings[step - 1]))
            if step < len(meetings):
                for target in meetings[step]:
                    pl.semaphore_signal(
                        meet_sem.at[step], inc=1, device_id=target, device_id_type=MESH
                    )
            taken.append(step)

    for load in loads[:2]:
        load.wait()
    csend[...] = cond[...].astype(jnp.bfloat16)
    iy = lax.broadcasted_iota(jnp.int32, (height, breadth), 0)
    iz = lax.broadcasted_iota(jnp.int32, (height, breadth), 1)
    flat = iy * breadth + iz

    def y_up(f):
        return jnp.where(iy == height - 1, 0.0, pltpu.roll(f, height - 1, 0))

    def y_down(f):
        return jnp.where(iy == 0, 0.0, pltpu.roll(f, 1, 0))

    def z_up(f):
        return jnp.where(iz == breadth - 1, 0.0, pltpu.roll(f, breadth - 1, 1))

    def z_down(f):
        return jnp.where(iz == 0, 0.0, pltpu.roll(f, 1, 1))

    def pack(i, carry):
        s, p = i // 2, i % 2
        for plane in range(depth):
            for c in range(3):
                send[plane, c, i] = warm[s, p, c, plane].astype(jnp.bfloat16)
        ex = warm[s, p, 0, 0]
        mix[0, i] = (warm[s, p, 1, 0] + (y_up(ex) - ex)).astype(jnp.bfloat16)
        mix[1, i] = (warm[s, p, 2, 0] + (z_up(ex) - ex)).astype(jnp.bfloat16)
        return carry

    lax.fori_loop(0, 2 * count, pack, 0)
    pl.semaphore_wait(barrier, len(partners))

    def halo(k, way, target, source, place):
        return pltpu.make_async_remote_copy(
            source,
            place,
            send_sem.at[way, k],
            recv_sem.at[way, k],
            device_id=target,
            device_id_type=MESH,
        )

    last = depth - 1
    far = [
        halo(last, 0, after, mix, land.at[0, 0, pl.ds(1, 2)]),
        halo(last, 1, before, send.at[last, pl.ds(1, 2)], land.at[1, last, pl.ds(1, 2)]),
    ]
    inner = [
        [
            halo(k, 0, after, send.at[last - k], land.at[0, last - k]),
            halo(k, 1, before, send.at[k], land.at[1, k]),
        ]
        for k in range(last)
    ]
    coefs = [
        halo(depth, 0, after, csend.at[pl.ds(1, last)], cland.at[0, pl.ds(1, last)]),
        halo(depth, 1, before, csend.at[pl.ds(0, last)], cland.at[1, pl.ds(0, last)]),
    ]
    stages = [inner[0] + coefs] + inner[1:] + [far]
    for stage in stages:
        for copy in stage:
            copy.start()
    meet(1)

    for load in loads[2:]:
        load.wait()
    has_before = (me > 0).astype(jnp.float32)
    has_after = (me < peers - 1).astype(jnp.float32)
    def angular_of(s):
        k = freq[group[s]]
        low = jnp.where(k % 2 == 1, jnp.float32(1.25), jnp.float32(1.0))
        mid = jnp.where((k // 2) % 2 == 1, jnp.float32(1.25**2), jnp.float32(1.0))
        top = jnp.where((k // 4) % 2 == 1, jnp.float32(1.25**4), jnp.float32(1.0))
        return 0.25 * (low * mid * top)

    def guard(plane, f):
        if plane < depth:
            return f * has_before
        if plane >= 2 * depth:
            return f * has_after
        return f

    def start_plane(s, p, c, plane):
        if plane < depth:
            return guard(plane, land[0, plane, c, 2 * s + p].astype(jnp.float32))
        if plane >= 2 * depth:
            return guard(plane, land[1, plane - 2 * depth, c, 2 * s + p].astype(jnp.float32))
        return warm[s, p, c, plane - depth]

    def cond_plane(plane):
        if plane < depth:
            return cland[0, plane].astype(jnp.float32)
        if plane >= 2 * depth:
            return cland[1, plane - 2 * depth].astype(jnp.float32)
        return cond[plane - depth]

    def stored(buffer):
        return lambda s, p, c, plane: buffer[2 * s + p, c, plane]

    def sweep(source, target, *spans):
        def one(i, carry):
            s, p = i // 2, i % 2
            turn = (1 - 2 * p).astype(jnp.float32) * (RELAX * angular_of(s))
            for low, high in spans:
                span(s, p, i, turn, low, high)
            return carry

        def span(s, p, i, turn, low, high):
            old = {
                (c, plane): source(s, p, c, plane)
                for plane in range(low - 1, high + 1)
                for c in range(3)
                if plane not in (0, 3 * depth - 1) or c > 0
            }

            def mag_y(plane):
                return (z_up(old[0, plane]) - old[0, plane]) - (old[2, plane + 1] - old[2, plane])

            def mag_z(plane):
                return (old[1, plane + 1] - old[1, plane]) - (y_up(old[0, plane]) - old[0, plane])

            if low == 1:
                hy_low, hz_low = old[2, 0] - old[2, 1], old[1, 1] - old[1, 0]
            else:
                hy_low, hz_low = mag_y(low - 1), mag_z(low - 1)
            for plane in range(low, high):
                ey, ez = old[1, plane], old[2, plane]
                hx = (y_up(ez) - ez) - (z_up(ey) - ey)
                hy, hz = mag_y(plane), mag_z(plane)
                curl = (
                    (hz - y_down(hz)) - (hy - z_down(hy)),
                    (hx - z_down(hx)) - (hz - hz_low),
                    (hy - hy_low) - (hx - y_down(hx)),
                )
                hy_low, hz_low = hy, hz
                factor = turn * cond_plane(plane)
                here = cell[s] - (me * depth + plane - depth) * (height * breadth)
                point = flat == here
                for c in range(3):
                    other = source(s, 1 - p, c, plane)
                    term = jnp.where(point, RELAX * weight[s, p, c], 0.0)
                    new = old[c, plane] + term - RELAX * curl[c] + factor * other
                    target[i, c, plane] = guard(plane, new)

        lax.fori_loop(0, 2 * count, one, 0)

    iterates = [start_plane, stored(first), stored(second), stored(third)]
    buffers = [None, first, second, third]
    if depth > 2:
        sweep(iterates[0], buffers[1], (depth + 1, 2 * depth - 1))
    for k, stage in enumerate(stages):
        for copy in stage:
            copy.wait_recv()
        for it in range(1, k + 2):
            reached = k + 1 - it
            low, high = depth - reached, 2 * depth + reached
            if it == k + 1:
                inside = (low + 1, high - 1) if it == 1 and depth > 2 else None
                if inside is None:
                    sweep(iterates[it - 1], buffers[it], (low, high))
                else:
                    sweep(iterates[it - 1], buffers[it], (low, low + 1), (high - 1, high))
            else:
                sweep(iterates[it - 1], buffers[it], (low, low + 1), (high - 1, high))

    meet(2)

    def products(s, carry):
        g = group[s]
        angular = angular_of(s)
        for plane in range(depth):
            real = jnp.zeros((height, breadth), jnp.float32)
            imag = jnp.zeros((height, breadth), jnp.float32)
            for c in range(3):
                fr, fi = back[g, 0, c, plane], back[g, 1, c, plane]
                ar, ai = third[2 * s, c, depth + plane], third[2 * s + 1, c, depth + plane]
                real += fr * ar - fi * ai
                imag += fr * ai + fi * ar
            coef = angular * cond[plane]
            rows[rx, plane, 2 * s] = (coef * real).astype(jnp.bfloat16)
            rows[rx, plane, 2 * s + 1] = (coef * imag).astype(jnp.bfloat16)
        return carry

    lax.fori_loop(0, count, products, 0)

    edges = [
        pltpu.make_async_remote_copy(
            rows.at[rx, pl.ds(start, 2)],
            rland.at[way],
            rsend_sem.at[way],
            rrecv_sem.at[way],
            device_id=target,
            device_id_type=MESH,
        )
        for way, target, start in ((0, after, depth - 2), (1, before, 0))
    ]
    gather = [
        pltpu.make_async_remote_copy(
            rows.at[rx],
            rows.at[rx],
            gsend_sem.at[k],
            grecv_sem.at[k],
            device_id=target,
            device_id_type=MESH,
        )
        for k, target in enumerate(others)
    ]
    for copy in gather + edges:
        copy.start()
    meet(len(meetings))
    for copy in edges:
        copy.wait_recv()

    def smoothing(r, carry):
        planes = (
            [rland[0, k, r].astype(jnp.float32) * has_before for k in range(2)]
            + [rows[rx, k, r].astype(jnp.float32) for k in range(depth)]
            + [rland[1, k, r].astype(jnp.float32) * has_after for k in range(2)]
        )
        for step in range(2):
            ends = [planes[0], planes[-1]]
            planes = [
                planes[k]
                + KAPPA
                * (
                    planes[k - 1]
                    + planes[k + 1]
                    + y_up(planes[k])
                    + y_down(planes[k])
                    + z_up(planes[k])
                    + z_down(planes[k])
                    - 6.0 * planes[k]
                )
                for k in range(1, len(planes) - 1)
            ]
            if step == 0:
                planes[0] = planes[0] * has_before
                planes[-1] = planes[-1] * has_after
        for k in range(depth):
            smooth[r, k] = planes[k].astype(jnp.bfloat16)
        return carry

    lax.fori_loop(0, 2 * count, smoothing, 0)

    for copy in gather:
        copy.wait_recv()

    def dots(b, carry):
        peer, r = b // (2 * count), b % (2 * count)
        for a in range(2 * count):
            total = jnp.zeros((8, breadth), jnp.float32)
            for k in range(depth):
                product = smooth[a, k].astype(jnp.float32) * rows[peer, k, r].astype(jnp.float32)
                for j in range(height // 8):
                    total += product[8 * j : 8 * j + 8]
            sums[a, b] = jnp.sum(total, axis=0)
        return carry

    lax.fori_loop(0, 2 * count * rx_peers, dots, 0)
    ones = jnp.ones((8, breadth), jnp.float32)
    wide = 2 * count * rx_peers
    line_sums[column] = jnp.zeros(line_sums.shape[1:], jnp.float32)
    for a in range(2 * count):
        lanes = lax.dot_general(
            ones,
            sums[a],
            (((1,), (1,)), ((), ())),
            precision=lax.Precision.HIGHEST,
            preferred_element_type=jnp.float32,
        )
        line_sums[column, a : a + 1, 0:wide] = lanes[0:1]

    step_one = [
        pltpu.make_async_remote_copy(
            line_sums.at[column],
            line_sums.at[column],
            ssend_sem.at[0, k],
            srecv_sem.at[0, k],
            device_id=target,
            device_id_type=MESH,
        )
        for k, target in enumerate(along)
    ]
    meet(len(meetings) + 1)
    for copy in step_one:
        copy.start()
    for copy in step_one:
        copy.wait_recv()
    plane_sums[line] = jnp.sum(line_sums[...], axis=0)
    step_two = [
        pltpu.make_async_remote_copy(
            plane_sums.at[line],
            plane_sums.at[line],
            ssend_sem.at[1, k],
            srecv_sem.at[1, k],
            device_id=target,
            device_id_type=MESH,
        )
        for k, target in enumerate(across)
    ]
    for copy in step_two:
        copy.start()
    for copy in step_two:
        copy.wait_recv()
    total = jnp.sum(plane_sums[...], axis=0)
    cells = depth * height * breadth * peers
    block_ref[...] = total[0 : 2 * count, 0:wide] / cells
    for copy in sum(stages, []) + edges + gather + step_one + step_two:
        copy.wait_send()


def shards(conductivity, background, warm_start, data_weight, recv_cell, src_group, group_freq):
    count = warm_start.shape[0]
    depth, height, breadth = conductivity.shape
    peers, rx_peers = lax.axis_size("space"), lax.axis_size("rx")
    lines = 1
    while lines * lines < peers:
        lines *= 2
    columns = peers // lines
    rows = 2 * count
    wide = rows * rx_peers
    plane = (height, breadth)
    f32, b16 = jnp.float32, jnp.bfloat16
    vmem, dma = pltpu.VMEM, pltpu.SemaphoreType.DMA
    hbm = pl.BlockSpec(memory_space=pltpu.HBM)
    operands = (
        conductivity,
        background,
        warm_start,
        data_weight,
        recv_cell,
        src_group,
        group_freq,
    )
    pinned = [pltpu.with_memory_space_constraint(x, pltpu.HBM) for x in operands]
    block, smoothed = pl.pallas_call(
        functools.partial(kernel, peers, lines, rx_peers),
        name="inversion_step",
        out_shape=(
            pltpu.VMEM((rows, wide), f32),
            pltpu.VMEM((rows, depth) + plane, b16),
        ),
        in_specs=[hbm] * 7,
        out_specs=(pl.BlockSpec(memory_space=vmem), pl.BlockSpec(memory_space=vmem)),
        scratch_shapes=[
            vmem(conductivity.shape, f32),
            vmem(background.shape, f32),
            vmem(warm_start.shape, f32),
            pltpu.SMEM(data_weight.shape, f32),
            pltpu.SMEM(recv_cell.shape, jnp.int32),
            pltpu.SMEM(src_group.shape, jnp.int32),
            pltpu.SMEM(group_freq.shape, jnp.int32),
            vmem((depth, 3, rows) + plane, b16),
            vmem((2, rows) + plane, b16),
            vmem((depth,) + plane, b16),
            vmem((2, depth, 3, rows) + plane, b16),
            vmem((2, depth) + plane, b16),
            vmem((rows, 3, 3 * depth) + plane, f32),
            vmem((rows, 3, 3 * depth) + plane, f32),
            vmem((rows, 3, 3 * depth) + plane, f32),
            vmem((rx_peers, depth, rows) + plane, b16),
            vmem((2, 2, rows) + plane, b16),
            vmem((rows, wide, breadth), f32),
            vmem((columns, 8, 128), f32),
            vmem((lines, 8, 128), f32),
            dma((7,)),
            dma((2, depth + 1)),
            dma((2, depth + 1)),
            dma((2,)),
            dma((2,)),
            dma((rx_peers - 1,)),
            dma((rx_peers - 1,)),
            dma((2, max(lines, columns) - 1)),
            dma((2, max(lines, columns) - 1)),
            pltpu.SemaphoreType.REGULAR((4,)),
        ],
        compiler_params=pltpu.CompilerParams(
            collective_id=0, has_side_effects=True, vmem_limit_bytes=48 * 2**20
        ),
    )(*pinned)
    return block, smoothed.reshape((count, 2, depth) + plane)


def solution(mesh):
    in_specs = (
        P("space", None, None),
        P(None, None, None, "space", None, None),
        P("rx", None, None, "space", None, None),
        P("rx", None, None),
        P("rx"),
        P("rx"),
        P(),
    )
    out_specs = (P("rx", None), P("rx", None, "space", None, None))
    return jax.shard_map(shards, mesh=mesh, in_specs=in_specs, out_specs=out_specs, check_vma=False)
```

```python
import functools

import jax
import jax.numpy as jnp
from jax import lax
from jax.experimental import pallas as pl
from jax.experimental.pallas import tpu as pltpu
from jax.sharding import PartitionSpec as P

ITERS = 3
RELAX = 0.2
KAPPA = 0.1
MESH = pl.DeviceIdType.MESH


def kernel(
    peers,
    lines,
    rx_peers,
    cond_hbm,
    back_hbm,
    warm_hbm,
    weight_hbm,
    cell_hbm,
    group_hbm,
    freq_hbm,
    block_ref,
    smooth,
    cond,
    back,
    warm,
    weight,
    cell,
    group,
    freq,
    send,
    land,
    cland,
    alone_1,
    alone_2,
    alone_3,
    delta_1,
    delta_2,
    delta_3,
    echo,
    reply,
    extra,
    rows,
    rland,
    sums,
    line_sums,
    plane_sums,
    load_sem,
    send_sem,
    recv_sem,
    rsend_sem,
    rrecv_sem,
    gsend_sem,
    grecv_sem,
    ssend_sem,
    srecv_sem,
    meet_sem,
):
    depth = cond.shape[0]
    height, breadth = cond.shape[1:]
    count = warm.shape[0]
    rx = lax.axis_index("rx")
    me = lax.axis_index("space")
    columns = peers // lines
    line = me // columns
    column = me % columns
    after = (rx, (me + 1) % peers)
    before = (rx, (me + peers - 1) % peers)
    others = [((rx + k) % rx_peers, me) for k in range(1, rx_peers)]

    def at(line, column):
        return (rx, (line % lines) * columns + column % columns)

    along = [at(line, column + k) for k in range(1, columns)]
    across = [at(line + k, column) for k in range(1, lines)]
    rows_y = lines // 2
    half = (line // rows_y) * rows_y

    def beside(k):
        return at(half + (line + k + rows_y) % rows_y, column)

    opposite = at(line + rows_y, column)

    loads = [
        pltpu.make_async_copy(src, dst, load_sem.at[i])
        for i, (src, dst) in enumerate(
            (
                (warm_hbm, warm),
                (cond_hbm, cond),
                (weight_hbm, weight),
                (cell_hbm, cell),
                (group_hbm, group),
                (freq_hbm, freq),
                (back_hbm, back),
            )
        )
    ]
    for load in loads:
        load.start()
    barrier = pltpu.get_barrier_semaphore()
    near = [at(line, column + 1), at(line, column - 1), opposite]
    if rows_y > 1:
        near += [beside(1), beside(-1)]
    partners = [before, after] + near + others
    for partner in partners:
        pl.semaphore_signal(barrier, inc=1, device_id=partner, device_id_type=MESH)

    meetings = []
    reach, y_steps = 1, 0
    while reach < max(columns, rows_y) // 2:
        targets = []
        if reach < columns // 2:
            targets += [at(line, column + reach), at(line, column - reach)]
        if reach < rows_y // 2:
            targets += [beside(reach), beside(-reach)]
            y_steps += 1
        meetings.append(targets)
        reach *= 2
    if len(meetings) == y_steps:
        meetings.append([])
    meetings[y_steps].append(opposite)
    taken = []

    def meet(steps):
        while len(taken) < min(steps, len(meetings) + 1):
            step = len(taken)
            if step > 0:
                pl.semaphore_wait(meet_sem.at[step - 1], len(meetings[step - 1]))
            if step < len(meetings):
                for target in meetings[step]:
                    pl.semaphore_signal(
                        meet_sem.at[step], inc=1, device_id=target, device_id_type=MESH
                    )
            taken.append(step)

    for load in loads[:2]:
        load.wait()
    iy = lax.broadcasted_iota(jnp.int32, (height, breadth), 0)
    iz = lax.broadcasted_iota(jnp.int32, (height, breadth), 1)
    flat = iy * breadth + iz

    def y_up(f):
        return jnp.where(iy == height - 1, 0.0, pltpu.roll(f, height - 1, 0))

    def y_down(f):
        return jnp.where(iy == 0, 0.0, pltpu.roll(f, 1, 0))

    def z_up(f):
        return jnp.where(iz == breadth - 1, 0.0, pltpu.roll(f, breadth - 1, 1))

    def z_down(f):
        return jnp.where(iz == 0, 0.0, pltpu.roll(f, 1, 1))

    def outflow(k, i, first_plane, last_plane):
        ex, ey, ez = last_plane
        send[k, 0, 0, i] = (ey + (y_up(ex) - ex)).astype(jnp.bfloat16)
        send[k, 0, 1, i] = (ez + (z_up(ex) - ex)).astype(jnp.bfloat16)
        send[k, 1, 0, i] = first_plane[1].astype(jnp.bfloat16)
        send[k, 1, 1, i] = first_plane[2].astype(jnp.bfloat16)

    def pack(i, carry):
        s, p = i // 2, i % 2
        outflow(0, i, [warm[s, p, c, 0] for c in range(3)], [warm[s, p, c, last] for c in range(3)])
        return carry

    last = depth - 1
    lax.fori_loop(0, 2 * count, pack, 0, unroll=2)
    pl.semaphore_wait(barrier, len(partners))

    def halo(k, way, source, place):
        return pltpu.make_async_remote_copy(
            source,
            place,
            send_sem.at[way, k],
            recv_sem.at[way, k],
            device_id=(after, before)[way],
            device_id_type=MESH,
        )

    flows = [[halo(k, way, send.at[k, way], land.at[k, way]) for way in (0, 1)] for k in range(ITERS)]
    coefs = [halo(ITERS, 0, cond.at[last], cland.at[0]), halo(ITERS, 1, cond.at[0], cland.at[1])]
    for copy in flows[0] + coefs:
        copy.start()
    meet(1)

    for load in loads[2:]:
        load.wait()
    has_before = (me > 0).astype(jnp.float32)
    has_after = (me < peers - 1).astype(jnp.float32)
    def angular_of(s):
        k = freq[group[s]]
        low = jnp.where(k % 2 == 1, jnp.float32(1.25), jnp.float32(1.0))
        mid = jnp.where((k // 2) % 2 == 1, jnp.float32(1.25**2), jnp.float32(1.0))
        top = jnp.where((k // 4) % 2 == 1, jnp.float32(1.25**4), jnp.float32(1.0))
        return 0.25 * (low * mid * top)

    def angular_of(s):
        k = freq[group[s]]
        low = jnp.where(k % 2 == 1, jnp.float32(1.25), jnp.float32(1.0))
        mid = jnp.where((k // 2) % 2 == 1, jnp.float32(1.25**2), jnp.float32(1.0))
        top = jnp.where((k // 4) % 2 == 1, jnp.float32(1.25**4), jnp.float32(1.0))
        return 0.25 * (low * mid * top)

    def guard(plane, f):
        if plane < depth:
            return f * has_before
        if plane >= 2 * depth:
            return f * has_after
        return f

    def start_plane(s, p, c, plane):
        if plane < depth:
            return guard(plane, land[0, plane, c, 2 * s + p].astype(jnp.float32))
        if plane >= 2 * depth:
            return guard(plane, land[1, plane - 2 * depth, c, 2 * s + p].astype(jnp.float32))
        return warm[s, p, c, plane - depth]

    def cond_plane(plane):
        if plane < depth:
            return cland[0, plane].astype(jnp.float32)
        if plane >= 2 * depth:
            return cland[1, plane - 2 * depth].astype(jnp.float32)
        return cond[plane - depth]

    def inflow_low(first_part, second_part, weight_):
        return (0.0, weight_ * first_part, weight_ * second_part)

    def inflow_high(ey, ez, weight_):
        div = (ey - y_down(ey)) + (ez - z_down(ez))
        return (-weight_ * div, weight_ * ey, weight_ * ez)

    def step(s, p, old, other, coef, with_source):
        turn = (1 - 2 * p).astype(jnp.float32) * (RELAX * angular_of(s))
        planes = len(old)
        hy_low, hz_low = -old[0][2], old[0][1]
        new = []
        for plane in range(planes):
            ex, ey, ez = old[plane]
            hx = (y_up(ez) - ez) - (z_up(ey) - ey)
            hy = (z_up(ex) - ex) + ez
            hz = (ex - y_up(ex)) - ey
            if plane < planes - 1:
                hy = hy - old[plane + 1][2]
                hz = hz + old[plane + 1][1]
            curl = (
                (hz - y_down(hz)) - (hy - z_down(hy)),
                (hx - z_down(hx)) - (hz - hz_low),
                (hy - hy_low) - (hx - y_down(hx)),
            )
            hy_low, hz_low = hy, hz
            factor = turn * coef(plane)
            fresh = [old[plane][c] - RELAX * curl[c] + factor * other(c, plane) for c in range(3)]
            if with_source:
                point = flat == cell[s] - (me * depth + plane) * (height * breadth)
                fresh = [
                    fresh[c] + jnp.where(point, RELAX * weight[s, p, c], 0.0) for c in range(3)
                ]
            new.append(fresh)
        return new

    def from_warm(i, c, plane):
        return warm[i // 2, i % 2, c, plane]

    def held(buffer):
        return lambda i, c, plane: buffer[i, c, plane]

    def sweep(source, target, with_source, send_slot=None):
        def one(i, carry):
            s, p = i // 2, i % 2
            old = [[source(i, c, plane) for c in range(3)] for plane in range(depth)]
            twin = i + 1 - 2 * p
            new = step(
                s, p, old, lambda c, plane: source(twin, c, plane), lambda k: cond[k], with_source
            )
            for plane in range(depth):
                for c in range(3):
                    target[i, c, plane] = new[plane][c]
            if send_slot is not None:
                outflow(send_slot, i, new[0], new[last])
            return carry

        lax.fori_loop(0, 2 * count, one, 0, unroll=2)

    sweep(from_warm, alone_1, True, 1)
    for copy in flows[1]:
        copy.start()
    sweep(held(alone_1), alone_2, True, 2)
    for copy in flows[2]:
        copy.start()
    sweep(held(alone_2), alone_3, True)

    def answer(i, carry):
        first_plane = [from_warm(i, c, 0) for c in range(3)]
        ex, ey, ez = [from_warm(i, c, last) for c in range(3)]
        low = inflow_high(first_plane[1], first_plane[2], RELAX)
        high = inflow_low(ey + (y_up(ex) - ex), ez + (z_up(ex) - ex), RELAX)
        echo[0, i, 0], echo[0, i, 1], echo[0, i, 2] = low
        echo[1, i, 0], echo[1, i, 1], echo[1, i, 2] = jnp.zeros_like(ex), high[1], high[2]
        extra[0, 0, 0, i] = low[1] + (y_up(low[0]) - low[0])
        extra[0, 0, 1, i] = low[2] + (z_up(low[0]) - low[0])
        extra[0, 1, 0, i] = high[1]
        extra[0, 1, 1, i] = high[2]
        return carry

    lax.fori_loop(0, 2 * count, answer, 0, unroll=2)
    for copy in coefs:
        copy.wait_recv()

    def answer_again(i, carry):
        s, p = i // 2, i % 2
        twin = i + 1 - 2 * p
        for way in range(2):
            new = step(
                s,
                p,
                [[echo[way, i, c] for c in range(3)]],
                lambda c, plane: echo[way, twin, c],
                lambda k: cland[way],
                False,
            )
            for c in range(3):
                reply[way, i, c] = new[0][c]
        return carry

    lax.fori_loop(0, 2 * count, answer_again, 0, unroll=2)

    weight_low, weight_high = RELAX * has_before, RELAX * has_after
    for copy in flows[0]:
        copy.wait_recv()
    meet(2)

    def arrival_0(i, carry):
        got = [[land[0, way, j, i].astype(jnp.float32) for j in range(2)] for way in range(2)]
        low = inflow_low(got[0][0], got[0][1], weight_low)
        high = inflow_high(got[1][0], got[1][1], weight_high)
        zero = jnp.zeros((height, breadth), jnp.float32)
        for c in range(3):
            delta_1[i, c, 0] = low[c] + zero
            delta_1[i, c, last] = high[c]
            for plane in range(1, last):
                delta_1[i, c, plane] = zero
        near = [alone_1[i, c, 0] + low[c] for c in range(3)]
        ex, ey, ez = [alone_1[i, c, last] + high[c] for c in range(3)]
        low = inflow_high(near[1], near[2], RELAX)
        low = [reply[0, i, c] + low[c] for c in range(3)]
        high = inflow_low(ey + (y_up(ex) - ex), ez + (z_up(ex) - ex), RELAX)
        extra[1, 0, 0, i] = low[1] + (y_up(low[0]) - low[0])
        extra[1, 0, 1, i] = low[2] + (z_up(low[0]) - low[0])
        extra[1, 1, 0, i] = reply[1, i, 1] + high[1]
        extra[1, 1, 1, i] = reply[1, i, 2] + high[2]
        return carry

    lax.fori_loop(0, 2 * count, arrival_0, 0, unroll=2)
    sweep(held(delta_1), delta_2, False)

    def total_inflow(k, i):
        got = [
            [land[k, way, j, i].astype(jnp.float32) + extra[k - 1, way, j, i] for j in range(2)]
            for way in range(2)
        ]
        low = inflow_low(got[0][0], got[0][1], weight_low)
        return low, inflow_high(got[1][0], got[1][1], weight_high)

    for copy in flows[1]:
        copy.wait_recv()

    def arrival_1(i, carry):
        low, high = total_inflow(1, i)
        for c in range(3):
            if c > 0:
                delta_2[i, c, 0] = delta_2[i, c, 0] + low[c]
            delta_2[i, c, last] = delta_2[i, c, last] + high[c]
        return carry

    lax.fori_loop(0, 2 * count, arrival_1, 0, unroll=2)
    sweep(held(delta_2), delta_3, False)

    slots = [0, last] + list(range(1, last))

    def product(s, plane, real_part, imag_part):
        g = group[s]
        angular = angular_of(s)
        real = jnp.zeros((height, breadth), jnp.float32)
        imag = jnp.zeros((height, breadth), jnp.float32)
        for c in range(3):
            fr, fi = back[g, 0, c, plane], back[g, 1, c, plane]
            real += fr * real_part[c] - fi * imag_part[c]
            imag += fr * imag_part[c] + fi * real_part[c]
        coef = angular * cond[plane]
        rows[rx, slots.index(plane), 2 * s] = (coef * real).astype(jnp.bfloat16)
        rows[rx, slots.index(plane), 2 * s + 1] = (coef * imag).astype(jnp.bfloat16)

    def swept(i, plane):
        return [alone_3[i, c, plane] + delta_3[i, c, plane] for c in range(3)]

    def inner_products(s, carry):
        for plane in range(1, last):
            product(s, plane, swept(2 * s, plane), swept(2 * s + 1, plane))
        return carry

    lax.fori_loop(0, count, inner_products, 0, unroll=2)

    def edge(part, way):
        plane = ((last - 1, 1), (last, 0))[part][way]
        place = ((0, 1), (1, 0))[part][way]
        return pltpu.make_async_remote_copy(
            rows.at[rx, slots.index(plane)],
            rland.at[way, place],
            rsend_sem.at[part, way],
            rrecv_sem.at[part, way],
            device_id=(after, before)[way],
            device_id_type=MESH,
        )

    def to_group(part, k):
        span = (pl.ds(2, depth - 2), pl.ds(0, 2))[part]
        return pltpu.make_async_remote_copy(
            rows.at[rx, span],
            rows.at[rx, span],
            gsend_sem.at[part, k],
            grecv_sem.at[part, k],
            device_id=others[k],
            device_id_type=MESH,
        )

    edges = [edge(part, way) for part in range(2) for way in range(2)]
    gather = [to_group(part, k) for part in range(2) for k in range(rx_peers - 1)]
    for copy in gather[: rx_peers - 1] + edges[:2]:
        copy.start()
    for copy in flows[2]:
        copy.wait_recv()

    def outer_products(s, carry):
        parts = []
        for i in (2 * s, 2 * s + 1):
            low, high = total_inflow(2, i)
            near, far = swept(i, 0), swept(i, last)
            parts.append(
                ([near[c] + low[c] for c in range(3)], [far[c] + high[c] for c in range(3)])
            )
        product(s, 0, parts[0][0], parts[1][0])
        product(s, last, parts[0][1], parts[1][1])
        return carry

    lax.fori_loop(0, count, outer_products, 0, unroll=2)
    for copy in gather[rx_peers - 1 :] + edges[2:]:
        copy.start()
    meet(len(meetings))
    for copy in edges:
        copy.wait_recv()

    def smoothing(r, carry):
        planes = (
            [rland[0, k, r].astype(jnp.float32) * has_before for k in range(2)]
            + [rows[rx, slots.index(k), r].astype(jnp.float32) for k in range(depth)]
            + [rland[1, k, r].astype(jnp.float32) * has_after for k in range(2)]
        )
        for step in range(2):
            ends = [planes[0], planes[-1]]
            planes = [
                planes[k]
                + KAPPA
                * (
                    planes[k - 1]
                    + planes[k + 1]
                    + y_up(planes[k])
                    + y_down(planes[k])
                    + z_up(planes[k])
                    + z_down(planes[k])
                    - 6.0 * planes[k]
                )
                for k in range(1, len(planes) - 1)
            ]
            if step == 0:
                planes[0] = planes[0] * has_before
                planes[-1] = planes[-1] * has_after
        for k in range(depth):
            smooth[r, k] = planes[k].astype(jnp.bfloat16)
        return carry

    lax.fori_loop(0, 2 * count, smoothing, 0, unroll=2)

    for copy in gather:
        copy.wait_recv()

    wide = 2 * count * rx_peers

    def dots(b, carry):
        peer, r = b // (2 * count), b % (2 * count)
        for a in range(2 * count):
            total = jnp.zeros((8, breadth), jnp.float32)
            for k in range(depth):
                left = smooth[a, k].astype(jnp.float32)
                product = left * rows[peer, slots.index(k), r].astype(jnp.float32)
                for j in range(height // 8):
                    total += product[8 * j : 8 * j + 8]
            sums[a, b] = jnp.sum(total, axis=0)
        return carry

    lax.fori_loop(0, wide, dots, 0)
    ones = jnp.ones((8, breadth), jnp.bfloat16)
    by_lane = sums[...].reshape(2 * count * wide, breadth)
    high = by_lane.astype(jnp.bfloat16)
    low = (by_lane - high.astype(jnp.float32)).astype(jnp.bfloat16)
    lanes = [
        lax.dot_general(
            ones, part, (((1,), (1,)), ((), ())), preferred_element_type=jnp.float32
        )
        for part in (high, low)
    ]
    line_sums[column] = jnp.zeros(line_sums.shape[1:], jnp.float32)
    line_sums[column, :, 0 : 2 * count * wide] = (lanes[0] + lanes[1])[0:1]

    step_one = [
        pltpu.make_async_remote_copy(
            line_sums.at[column],
            line_sums.at[column],
            ssend_sem.at[0, k],
            srecv_sem.at[0, k],
            device_id=target,
            device_id_type=MESH,
        )
        for k, target in enumerate(along)
    ]
    meet(len(meetings) + 1)
    for copy in step_one:
        copy.start()
    for copy in step_one:
        copy.wait_recv()
    plane_sums[line] = jnp.sum(line_sums[...], axis=0)
    step_two = [
        pltpu.make_async_remote_copy(
            plane_sums.at[line],
            plane_sums.at[line],
            ssend_sem.at[1, k],
            srecv_sem.at[1, k],
            device_id=target,
            device_id_type=MESH,
        )
        for k, target in enumerate(across)
    ]
    for copy in step_two:
        copy.start()
    for copy in step_two:
        copy.wait_recv()
    total = jnp.sum(plane_sums[...], axis=0)
    cells = depth * height * breadth * peers
    for a in range(2 * count):
        block_ref[a : a + 1, :] = total[:, a * wide : (a + 1) * wide] / cells
    for copy in sum(flows, []) + coefs + edges + gather + step_one + step_two:
        copy.wait_send()


def shards(conductivity, background, warm_start, data_weight, recv_cell, src_group, group_freq):
    count = warm_start.shape[0]
    depth, height, breadth = conductivity.shape
    peers, rx_peers = lax.axis_size("space"), lax.axis_size("rx")
    lines = 1
    while lines * lines < peers:
        lines *= 2
    columns = peers // lines
    rows = 2 * count
    wide = rows * rx_peers
    plane = (height, breadth)
    f32, b16 = jnp.float32, jnp.bfloat16
    vmem, dma = pltpu.VMEM, pltpu.SemaphoreType.DMA
    hbm = pl.BlockSpec(memory_space=pltpu.HBM)
    operands = (
        conductivity,
        background,
        warm_start,
        data_weight,
        recv_cell,
        src_group,
        group_freq,
    )
    pinned = [pltpu.with_memory_space_constraint(x, pltpu.HBM) for x in operands]
    block, smoothed = pl.pallas_call(
        functools.partial(kernel, peers, lines, rx_peers),
        name="inversion_step",
        out_shape=(
            pltpu.VMEM((rows, wide), f32),
            pltpu.VMEM((rows, depth) + plane, b16),
        ),
        in_specs=[hbm] * 7,
        out_specs=(pl.BlockSpec(memory_space=vmem), pl.BlockSpec(memory_space=vmem)),
        scratch_shapes=[
            vmem(conductivity.shape, f32),
            vmem(background.shape, f32),
            vmem(warm_start.shape, f32),
            pltpu.SMEM(data_weight.shape, f32),
            pltpu.SMEM(recv_cell.shape, jnp.int32),
            pltpu.SMEM(src_group.shape, jnp.int32),
            pltpu.SMEM(group_freq.shape, jnp.int32),
            vmem((ITERS, 2, 2, rows) + plane, b16),
            vmem((ITERS, 2, 2, rows) + plane, b16),
            vmem((2,) + plane, f32),
        ]
        + [vmem((rows, 3, depth) + plane, f32)] * 6
        + [vmem((2, rows, 3) + plane, f32)] * 2
        + [
            vmem((ITERS - 1, 2, 2, rows) + plane, f32),
            vmem((rx_peers, depth, rows) + plane, b16),
            vmem((2, 2, rows) + plane, b16),
            vmem((rows, wide, breadth), f32),
            vmem((columns, 1, breadth), f32),
            vmem((lines, 1, breadth), f32),
            dma((7,)),
            dma((2, ITERS + 1)),
            dma((2, ITERS + 1)),
            dma((2, 2)),
            dma((2, 2)),
            dma((2, rx_peers - 1)),
            dma((2, rx_peers - 1)),
            dma((2, max(lines, columns) - 1)),
            dma((2, max(lines, columns) - 1)),
            pltpu.SemaphoreType.REGULAR((4,)),
        ],
        compiler_params=pltpu.CompilerParams(
            collective_id=0, has_side_effects=True, vmem_limit_bytes=48 * 2**20
        ),
    )(*pinned)
    return block, smoothed.reshape((count, 2, depth) + plane)


def solution(mesh):
    in_specs = (
        P("space", None, None),
        P(None, None, None, "space", None, None),
        P("rx", None, None, "space", None, None),
        P("rx", None, None),
        P("rx"),
        P("rx"),
        P(),
    )
    out_specs = (P("rx", None), P("rx", None, "space", None, None))
    return jax.shard_map(shards, mesh=mesh, in_specs=in_specs, out_specs=out_specs, check_vma=False)
```

```python
import functools

import jax
import jax.numpy as jnp
from jax import lax
from jax.experimental import pallas as pl
from jax.experimental.pallas import tpu as pltpu
from jax.sharding import PartitionSpec as P

ITERS = 3
RELAX = 0.2
KAPPA = 0.1
MESH = pl.DeviceIdType.MESH


def kernel(
    peers,
    lines,
    rx_peers,
    cond_hbm,
    back_hbm,
    warm_hbm,
    weight_hbm,
    cell_hbm,
    group_hbm,
    freq_hbm,
    block_ref,
    smooth,
    cond,
    back,
    warm,
    weight,
    cell,
    group,
    freq,
    send,
    land,
    cland,
    alone_1,
    alone_2,
    alone_3,
    delta_1,
    delta_2,
    delta_3,
    echo,
    reply,
    extra,
    rows,
    rland,
    twice,
    sums,
    line_sums,
    plane_sums,
    load_sem,
    send_sem,
    recv_sem,
    rsend_sem,
    rrecv_sem,
    gsend_sem,
    grecv_sem,
    ssend_sem,
    srecv_sem,
    meet_sem,
):
    depth = cond.shape[0]
    height, breadth = cond.shape[1:]
    count = warm.shape[0]
    rx = lax.axis_index("rx")
    me = lax.axis_index("space")
    columns = peers // lines
    line = me // columns
    column = me % columns
    after = (rx, (me + 1) % peers)
    before = (rx, (me + peers - 1) % peers)
    others = []
    for k in range(0, rx_peers, 2):
        place = (rx + k) % rx_peers
        others += [(place, me)] * (k > 0) + [(place + 1 - 2 * (place % 2), me)]

    def at(line, column):
        return (rx, (line % lines) * columns + column % columns)

    along = [at(line, column + k) for k in range(1, columns)]
    across = [at(line + k, column) for k in range(1, lines)]
    rows_y = lines // 2
    half = (line // rows_y) * rows_y
    high_x = max(rx_peers // 2, 1)

    def beside(k):
        return at(half + (line + k + rows_y) % rows_y, column)

    def along_x(k):
        place = (2 * (rx // 2) + line // rows_y + k + 2 * high_x) % (2 * high_x)
        place_line = (place % 2) * rows_y + line % rows_y
        return (2 * (place // 2) + rx % 2, place_line * columns + column)

    opposite = at(line + rows_y, column)
    core = others[0]

    starts = [(s, p) for s in range(count) for p in range(2)]
    loads = [
        pltpu.make_async_copy(src, dst, load_sem.at[i])
        for i, (src, dst) in enumerate(
            [(warm_hbm.at[s, p], warm.at[s, p]) for s, p in starts]
            + [
                (cond_hbm, cond),
                (weight_hbm, weight),
                (cell_hbm, cell),
                (group_hbm, group),
                (freq_hbm, freq),
                (back_hbm, back),
            ]
        )
    ]
    barrier = pltpu.get_barrier_semaphore()
    ring_z = [at(line, column + 1), at(line, column - 1)]
    ring_x = [along_x(1), along_x(-1)]
    ring_y = [beside(1), beside(-1)] if rows_y > 1 else []
    partners = [before, after, core] + ring_z + ring_x + ring_y
    for partner in partners:
        pl.semaphore_signal(barrier, inc=1, device_id=partner, device_id_type=MESH)
    for load in loads[:-1]:
        load.start()

    meetings = [list(ring_x), [core], [opposite]]
    reach, k = 1, 0
    while reach < max(columns, rows_y) // 2:
        if k == len(meetings):
            meetings.append([])
        if reach < columns // 2:
            meetings[k] += [at(line, column + reach), at(line, column - reach)]
        if reach < rows_y // 2:
            meetings[k] += [beside(reach), beside(-reach)]
        reach, k = 2 * reach, k + 1
    taken = []

    def meet(steps):
        while len(taken) < min(steps, len(meetings) + 1):
            step = len(taken)
            if step > 0:
                pl.semaphore_wait(meet_sem.at[step - 1], len(meetings[step - 1]))
            if step < len(meetings):
                for target in meetings[step]:
                    pl.semaphore_signal(
                        meet_sem.at[step], inc=1, device_id=target, device_id_type=MESH
                    )
            taken.append(step)

    for load in loads[: len(starts) + 1]:
        load.wait()
    iy = lax.broadcasted_iota(jnp.int32, (height, breadth), 0)
    iz = lax.broadcasted_iota(jnp.int32, (height, breadth), 1)
    flat = iy * breadth + iz

    def y_up(f):
        return jnp.where(iy == height - 1, 0.0, pltpu.roll(f, height - 1, 0))

    def y_down(f):
        return jnp.where(iy == 0, 0.0, pltpu.roll(f, 1, 0))

    def z_up(f):
        return jnp.where(iz == breadth - 1, 0.0, pltpu.roll(f, breadth - 1, 1))

    def z_down(f):
        return jnp.where(iz == 0, 0.0, pltpu.roll(f, 1, 1))

    def outflow(k, i, first_plane, last_plane):
        ex, ey, ez = last_plane
        send[k, 0, 0, i] = (ey + (y_up(ex) - ex)).astype(jnp.bfloat16)
        send[k, 0, 1, i] = (ez + (z_up(ex) - ex)).astype(jnp.bfloat16)
        send[k, 1, 0, i] = first_plane[1].astype(jnp.bfloat16)
        send[k, 1, 1, i] = first_plane[2].astype(jnp.bfloat16)

    def pack(i, carry):
        s, p = i // 2, i % 2
        outflow(0, i, [warm[s, p, c, 0] for c in range(3)], [warm[s, p, c, last] for c in range(3)])
        return carry

    last = depth - 1
    lax.fori_loop(0, 2 * count, pack, 0, unroll=2)
    pl.semaphore_wait(barrier, len(partners))

    def halo(k, way, source, place):
        return pltpu.make_async_remote_copy(
            source,
            place,
            send_sem.at[way, k],
            recv_sem.at[way, k],
            device_id=(after, before)[way],
            device_id_type=MESH,
        )

    flows = [[halo(k, way, send.at[k, way], land.at[k, way]) for way in (0, 1)] for k in range(ITERS)]
    coefs = [halo(ITERS, 0, cond.at[last], cland.at[0]), halo(ITERS, 1, cond.at[0], cland.at[1])]
    for copy in flows[0] + coefs:
        copy.start()
    loads[-1].start()
    meet(1)

    for load in loads[len(starts) + 1 : -1]:
        load.wait()
    has_before = (me > 0).astype(jnp.float32)
    has_after = (me < peers - 1).astype(jnp.float32)
    def angular_of(s):
        k = freq[group[s]]
        low = jnp.where(k % 2 == 1, jnp.float32(1.25), jnp.float32(1.0))
        mid = jnp.where((k // 2) % 2 == 1, jnp.float32(1.25**2), jnp.float32(1.0))
        top = jnp.where((k // 4) % 2 == 1, jnp.float32(1.25**4), jnp.float32(1.0))
        return 0.25 * (low * mid * top)

    def angular_of(s):
        k = freq[group[s]]
        low = jnp.where(k % 2 == 1, jnp.float32(1.25), jnp.float32(1.0))
        mid = jnp.where((k // 2) % 2 == 1, jnp.float32(1.25**2), jnp.float32(1.0))
        top = jnp.where((k // 4) % 2 == 1, jnp.float32(1.25**4), jnp.float32(1.0))
        return 0.25 * (low * mid * top)

    def guard(plane, f):
        if plane < depth:
            return f * has_before
        if plane >= 2 * depth:
            return f * has_after
        return f

    def start_plane(s, p, c, plane):
        if plane < depth:
            return guard(plane, land[0, plane, c, 2 * s + p].astype(jnp.float32))
        if plane >= 2 * depth:
            return guard(plane, land[1, plane - 2 * depth, c, 2 * s + p].astype(jnp.float32))
        return warm[s, p, c, plane - depth]

    def cond_plane(plane):
        if plane < depth:
            return cland[0, plane].astype(jnp.float32)
        if plane >= 2 * depth:
            return cland[1, plane - 2 * depth].astype(jnp.float32)
        return cond[plane - depth]

    def inflow_low(first_part, second_part, weight_):
        return (0.0, weight_ * first_part, weight_ * second_part)

    def inflow_high(ey, ez, weight_):
        div = (ey - y_down(ey)) + (ez - z_down(ez))
        return (-weight_ * div, weight_ * ey, weight_ * ez)

    def step(s, p, old, other, coef, with_source):
        turn = (1 - 2 * p).astype(jnp.float32) * (RELAX * angular_of(s))
        planes = len(old)
        hy_low, hz_low = -old[0][2], old[0][1]
        new = []
        for plane in range(planes):
            ex, ey, ez = old[plane]
            hx = (y_up(ez) - ez) - (z_up(ey) - ey)
            hy = (z_up(ex) - ex) + ez
            hz = (ex - y_up(ex)) - ey
            if plane < planes - 1:
                hy = hy - old[plane + 1][2]
                hz = hz + old[plane + 1][1]
            curl = (
                (hz - y_down(hz)) - (hy - z_down(hy)),
                (hx - z_down(hx)) - (hz - hz_low),
                (hy - hy_low) - (hx - y_down(hx)),
            )
            hy_low, hz_low = hy, hz
            factor = turn * coef(plane)
            fresh = [old[plane][c] - RELAX * curl[c] + factor * other(c, plane) for c in range(3)]
            if with_source:
                point = flat == cell[s] - (me * depth + plane) * (height * breadth)
                fresh = [
                    fresh[c] + jnp.where(point, RELAX * weight[s, p, c], 0.0) for c in range(3)
                ]
            new.append(fresh)
        return new

    def from_warm(i, c, plane):
        return warm[i // 2, i % 2, c, plane]

    def held(buffer):
        return lambda i, c, plane: buffer[i, c, plane]

    def sweep(source, target, with_source, send_slot=None):
        def one(i, carry):
            s, p = i // 2, i % 2
            old = [[source(i, c, plane) for c in range(3)] for plane in range(depth)]
            twin = i + 1 - 2 * p
            new = step(
                s, p, old, lambda c, plane: source(twin, c, plane), lambda k: cond[k], with_source
            )
            for plane in range(depth):
                for c in range(3):
                    target[i, c, plane] = new[plane][c]
            if send_slot is not None:
                outflow(send_slot, i, new[0], new[last])
            return carry

        lax.fori_loop(0, 2 * count, one, 0, unroll=2)

    sweep(from_warm, alone_1, True, 1)
    for copy in flows[1]:
        copy.start()
    sweep(held(alone_1), alone_2, True, 2)
    for copy in flows[2]:
        copy.start()
    sweep(held(alone_2), alone_3, True)

    def answer(i, carry):
        first_plane = [from_warm(i, c, 0) for c in range(3)]
        ex, ey, ez = [from_warm(i, c, last) for c in range(3)]
        low = inflow_high(first_plane[1], first_plane[2], RELAX)
        high = inflow_low(ey + (y_up(ex) - ex), ez + (z_up(ex) - ex), RELAX)
        echo[0, i, 0], echo[0, i, 1], echo[0, i, 2] = low
        echo[1, i, 0], echo[1, i, 1], echo[1, i, 2] = jnp.zeros_like(ex), high[1], high[2]
        extra[0, 0, 0, i] = low[1] + (y_up(low[0]) - low[0])
        extra[0, 0, 1, i] = low[2] + (z_up(low[0]) - low[0])
        extra[0, 1, 0, i] = high[1]
        extra[0, 1, 1, i] = high[2]
        return carry

    lax.fori_loop(0, 2 * count, answer, 0, unroll=2)
    meet(2)
    for copy in coefs:
        copy.wait_recv()

    def answer_again(i, carry):
        s, p = i // 2, i % 2
        twin = i + 1 - 2 * p
        for way in range(2):
            new = step(
                s,
                p,
                [[echo[way, i, c] for c in range(3)]],
                lambda c, plane: echo[way, twin, c],
                lambda k: cland[way],
                False,
            )
            for c in range(3):
                reply[way, i, c] = new[0][c]
        return carry

    lax.fori_loop(0, 2 * count, answer_again, 0, unroll=2)

    weight_low, weight_high = RELAX * has_before, RELAX * has_after
    for copy in flows[0]:
        copy.wait_recv()

    def arrival_0(i, carry):
        got = [[land[0, way, j, i].astype(jnp.float32) for j in range(2)] for way in range(2)]
        low = inflow_low(got[0][0], got[0][1], weight_low)
        high = inflow_high(got[1][0], got[1][1], weight_high)
        zero = jnp.zeros((height, breadth), jnp.float32)
        for c in range(3):
            delta_1[i, c, 0] = low[c] + zero
            delta_1[i, c, last] = high[c]
            for plane in range(1, last):
                delta_1[i, c, plane] = zero
        near = [alone_1[i, c, 0] + low[c] for c in range(3)]
        ex, ey, ez = [alone_1[i, c, last] + high[c] for c in range(3)]
        low = inflow_high(near[1], near[2], RELAX)
        low = [reply[0, i, c] + low[c] for c in range(3)]
        high = inflow_low(ey + (y_up(ex) - ex), ez + (z_up(ex) - ex), RELAX)
        extra[1, 0, 0, i] = low[1] + (y_up(low[0]) - low[0])
        extra[1, 0, 1, i] = low[2] + (z_up(low[0]) - low[0])
        extra[1, 1, 0, i] = reply[1, i, 1] + high[1]
        extra[1, 1, 1, i] = reply[1, i, 2] + high[2]
        return carry

    lax.fori_loop(0, 2 * count, arrival_0, 0, unroll=2)
    sweep(held(delta_1), delta_2, False)

    def total_inflow(k, i):
        got = [
            [land[k, way, j, i].astype(jnp.float32) + extra[k - 1, way, j, i] for j in range(2)]
            for way in range(2)
        ]
        low = inflow_low(got[0][0], got[0][1], weight_low)
        return low, inflow_high(got[1][0], got[1][1], weight_high)

    for copy in flows[1]:
        copy.wait_recv()

    def arrival_1(i, carry):
        low, high = total_inflow(1, i)
        for c in range(3):
            if c > 0:
                delta_2[i, c, 0] = delta_2[i, c, 0] + low[c]
            delta_2[i, c, last] = delta_2[i, c, last] + high[c]
        return carry

    lax.fori_loop(0, 2 * count, arrival_1, 0, unroll=2)
    sweep(held(delta_2), delta_3, False)

    slots = [0, last] + list(range(1, last))

    def product(s, plane, real_part, imag_part):
        g = group[s]
        angular = angular_of(s)
        real = jnp.zeros((height, breadth), jnp.float32)
        imag = jnp.zeros((height, breadth), jnp.float32)
        for c in range(3):
            fr, fi = back[g, 0, c, plane], back[g, 1, c, plane]
            real += fr * real_part[c] - fi * imag_part[c]
            imag += fr * imag_part[c] + fi * real_part[c]
        coef = angular * cond[plane]
        rows[rx, slots.index(plane), 2 * s] = (coef * real).astype(jnp.bfloat16)
        rows[rx, slots.index(plane), 2 * s + 1] = (coef * imag).astype(jnp.bfloat16)

    def swept(i, plane):
        return [alone_3[i, c, plane] + delta_3[i, c, plane] for c in range(3)]

    def inner_products(s, carry):
        for plane in range(1, last):
            product(s, plane, swept(2 * s, plane), swept(2 * s + 1, plane))
        return carry

    loads[-1].wait()
    lax.fori_loop(0, count, inner_products, 0, unroll=2)

    def edge(part, way):
        plane = ((last - 1, 1), (last, 0))[part][way]
        place = ((0, 1), (1, 0))[part][way]
        return pltpu.make_async_remote_copy(
            rows.at[rx, slots.index(plane)],
            rland.at[way, place],
            rsend_sem.at[part, way],
            rrecv_sem.at[part, way],
            device_id=(after, before)[way],
            device_id_type=MESH,
        )

    def to_group(part, k):
        span = (pl.ds(2, depth - 2), pl.ds(0, 2))[part]
        return pltpu.make_async_remote_copy(
            rows.at[rx, span],
            rows.at[rx, span],
            gsend_sem.at[part, k],
            grecv_sem.at[part, k],
            device_id=others[k],
            device_id_type=MESH,
        )

    edges = [edge(part, way) for part in range(2) for way in range(2)]
    gather = [to_group(part, k) for part in range(2) for k in range(rx_peers - 1)]
    meet(3)
    for copy in gather[: rx_peers - 1] + edges[:2]:
        copy.start()
    for copy in flows[2]:
        copy.wait_recv()

    def outer_products(s, carry):
        parts = []
        for i in (2 * s, 2 * s + 1):
            low, high = total_inflow(2, i)
            near, far = swept(i, 0), swept(i, last)
            parts.append(
                ([near[c] + low[c] for c in range(3)], [far[c] + high[c] for c in range(3)])
            )
        product(s, 0, parts[0][0], parts[1][0])
        product(s, last, parts[0][1], parts[1][1])
        return carry

    lax.fori_loop(0, count, outer_products, 0, unroll=2)
    for copy in gather[rx_peers - 1 :] + edges[2:]:
        copy.start()
    def within(f):
        return f + KAPPA * (y_up(f) + y_down(f) + z_up(f) + z_down(f) - 6.0 * f)

    def smooth_own(r, carry):
        own = [rows[rx, slots.index(k), r].astype(jnp.float32) for k in range(depth)]
        once = [within(f) for f in own]
        for k in range(depth):
            if k > 0:
                once[k] += KAPPA * own[k - 1]
            if k < last:
                once[k] += KAPPA * own[k + 1]
        once = [(KAPPA * has_before) * own[0]] + once + [(KAPPA * has_after) * own[last]]
        for k in range(depth):
            twice[r, k] = within(once[k + 1]) + KAPPA * (once[k] + once[k + 2])
        return carry

    lax.fori_loop(0, 2 * count, smooth_own, 0, unroll=2)
    for copy in edges:
        copy.wait_recv()

    def smooth_edges(r, carry):
        value = [twice[r, k] for k in range(depth)]
        for has, ends, border, inner in (
            (has_before, (0, 1), 0, 1),
            (has_after, (1, 0), last, last - 1),
        ):
            way = 0 if border == 0 else 1
            far, near = (rland[way, k, r].astype(jnp.float32) * has for k in ends)
            value[border] += (2.0 * KAPPA) * within(near) + (KAPPA * KAPPA) * far
            value[inner] += (KAPPA * KAPPA) * near
        for k in range(depth):
            rounded = value[k].astype(jnp.bfloat16)
            smooth[r, k] = rounded
            twice[r, k] = rounded.astype(jnp.float32)
        return carry

    lax.fori_loop(0, 2 * count, smooth_edges, 0, unroll=2)

    for copy in gather[:: rx_peers - 1]:
        copy.wait_recv()

    wide = 2 * count * rx_peers

    def dots(b, carry):
        peer, r = (rx - rx % 2 + b // (2 * count)) % rx_peers, b % (2 * count)
        right = [rows[peer, slots.index(k), r].astype(jnp.float32) for k in range(depth)]
        for a in range(2 * count):
            total = jnp.zeros((8, breadth), jnp.float32)
            for k in range(depth):
                product = twice[a, k] * right[k]
                for j in range(height // 8):
                    total += product[8 * j : 8 * j + 8]
            sums[a, peer * (2 * count) + r] = jnp.sum(total, axis=0)
        return carry

    lax.fori_loop(0, 4 * count, dots, 0, unroll=2)
    for k in range(1, rx_peers - 1):
        for copy in gather[k :: rx_peers - 1]:
            copy.wait_recv()
    lax.fori_loop(4 * count, wide, dots, 0, unroll=2)
    ones = jnp.ones((8, breadth), jnp.bfloat16)
    by_lane = sums[...].reshape(2 * count * wide, breadth)
    high = by_lane.astype(jnp.bfloat16)
    low = (by_lane - high.astype(jnp.float32)).astype(jnp.bfloat16)
    lanes = [
        lax.dot_general(
            ones, part, (((1,), (1,)), ((), ())), preferred_element_type=jnp.float32
        )
        for part in (high, low)
    ]
    line_sums[column] = jnp.zeros(line_sums.shape[1:], jnp.float32)
    line_sums[column, :, 0 : 2 * count * wide] = (lanes[0] + lanes[1])[0:1]

    step_one = [
        pltpu.make_async_remote_copy(
            line_sums.at[column],
            line_sums.at[column],
            ssend_sem.at[0, k],
            srecv_sem.at[0, k],
            device_id=target,
            device_id_type=MESH,
        )
        for k, target in enumerate(along)
    ]
    meet(len(meetings) + 1)
    for copy in step_one:
        copy.start()
    for copy in step_one:
        copy.wait_recv()
    plane_sums[line] = jnp.sum(line_sums[...], axis=0)
    step_two = [
        pltpu.make_async_remote_copy(
            plane_sums.at[line],
            plane_sums.at[line],
            ssend_sem.at[1, k],
            srecv_sem.at[1, k],
            device_id=target,
            device_id_type=MESH,
        )
        for k, target in enumerate(across)
    ]
    for copy in step_two:
        copy.start()
    for copy in step_two:
        copy.wait_recv()
    total = jnp.sum(plane_sums[...], axis=0)
    cells = depth * height * breadth * peers
    for a in range(2 * count):
        block_ref[a : a + 1, :] = total[:, a * wide : (a + 1) * wide] / cells
    for copy in sum(flows, []) + coefs + edges + gather + step_one + step_two:
        copy.wait_send()


def deliver(block, smooth, block_out, smooth_out, sem):
    copies = [
        pltpu.make_async_copy(smooth, smooth_out, sem.at[0]),
        pltpu.make_async_copy(block, block_out, sem.at[1]),
    ]
    for copy in copies:
        copy.start()
    for copy in copies:
        copy.wait()


def shards(conductivity, background, warm_start, data_weight, recv_cell, src_group, group_freq):
    count = warm_start.shape[0]
    depth, height, breadth = conductivity.shape
    peers, rx_peers = lax.axis_size("space"), lax.axis_size("rx")
    lines = 1
    while lines * lines < peers:
        lines *= 2
    columns = peers // lines
    rows = 2 * count
    wide = rows * rx_peers
    plane = (height, breadth)
    f32, b16 = jnp.float32, jnp.bfloat16
    vmem, dma = pltpu.VMEM, pltpu.SemaphoreType.DMA
    hbm = pl.BlockSpec(memory_space=pltpu.HBM)
    operands = (
        conductivity,
        background,
        warm_start,
        data_weight,
        recv_cell,
        src_group,
        group_freq,
    )
    pinned = [pltpu.with_memory_space_constraint(x, pltpu.HBM) for x in operands]
    block, smoothed = pl.pallas_call(
        functools.partial(kernel, peers, lines, rx_peers),
        name="inversion_step",
        out_shape=(
            pltpu.VMEM((rows, wide), f32),
            pltpu.VMEM((rows, depth) + plane, b16),
        ),
        in_specs=[hbm] * 7,
        out_specs=(pl.BlockSpec(memory_space=vmem), pl.BlockSpec(memory_space=vmem)),
        scratch_shapes=[
            vmem(conductivity.shape, f32),
            vmem(background.shape, f32),
            vmem(warm_start.shape, f32),
            pltpu.SMEM(data_weight.shape, f32),
            pltpu.SMEM(recv_cell.shape, jnp.int32),
            pltpu.SMEM(src_group.shape, jnp.int32),
            pltpu.SMEM(group_freq.shape, jnp.int32),
            vmem((ITERS, 2, 2, rows) + plane, b16),
            vmem((ITERS, 2, 2, rows) + plane, b16),
            vmem((2,) + plane, f32),
        ]
        + [vmem((rows, 3, depth) + plane, f32)] * 6
        + [vmem((2, rows, 3) + plane, f32)] * 2
        + [
            vmem((ITERS - 1, 2, 2, rows) + plane, f32),
            vmem((rx_peers, depth, rows) + plane, b16),
            vmem((2, 2, rows) + plane, b16),
            vmem((rows, depth) + plane, f32),
            vmem((rows, wide, breadth), f32),
            vmem((columns, 1, breadth), f32),
            vmem((lines, 1, breadth), f32),
            dma((rows + 6,)),
            dma((2, ITERS + 1)),
            dma((2, ITERS + 1)),
            dma((2, 2)),
            dma((2, 2)),
            dma((2, rx_peers - 1)),
            dma((2, rx_peers - 1)),
            dma((2, max(lines, columns) - 1)),
            dma((2, max(lines, columns) - 1)),
            pltpu.SemaphoreType.REGULAR((3,)),
        ],
        compiler_params=pltpu.CompilerParams(
            collective_id=0, has_side_effects=True, vmem_limit_bytes=48 * 2**20
        ),
    )(*pinned)
    results = [pltpu.with_memory_space_constraint(x, vmem) for x in (block, smoothed)]
    block, smoothed = pl.pallas_call(
        deliver,
        name="deliver",
        out_shape=(pltpu.HBM((rows, wide), f32), pltpu.HBM((rows, depth) + plane, b16)),
        in_specs=[pl.BlockSpec(memory_space=vmem)] * 2,
        out_specs=(hbm, hbm),
        scratch_shapes=[dma((2,))],
    )(*results)
    return block, smoothed.reshape((count, 2, depth) + plane)


def solution(mesh):
    in_specs = (
        P("space", None, None),
        P(None, None, None, "space", None, None),
        P("rx", None, None, "space", None, None),
        P("rx", None, None),
        P("rx"),
        P("rx"),
        P(),
    )
    out_specs = (P("rx", None), P("rx", None, "space", None, None))
    return jax.shard_map(shards, mesh=mesh, in_specs=in_specs, out_specs=out_specs, check_vma=False)
```

```python
import functools

import jax
import jax.numpy as jnp
from jax import lax
from jax.experimental import pallas as pl
from jax.experimental.pallas import tpu as pltpu
from jax.sharding import PartitionSpec as P

ITERS = 3
RELAX = 0.2
KAPPA = 0.1
MESH = pl.DeviceIdType.MESH


def kernel(
    peers,
    lines,
    rx_peers,
    cond_hbm,
    back_hbm,
    warm_hbm,
    weight_hbm,
    cell_hbm,
    group_hbm,
    freq_hbm,
    block_ref,
    smooth,
    cond,
    back,
    warm,
    weight,
    cell,
    group,
    freq,
    send,
    land,
    cland,
    alone_1,
    alone_2,
    alone_3,
    delta_1,
    delta_2,
    delta_3,
    echo,
    reply,
    extra,
    rows,
    rland,
    twice,
    sums,
    line_sums,
    plane_sums,
    load_sem,
    send_sem,
    recv_sem,
    rsend_sem,
    rrecv_sem,
    gsend_sem,
    grecv_sem,
    ssend_sem,
    srecv_sem,
    meet_sem,
):
    depth = cond.shape[0]
    height, breadth = cond.shape[1:]
    count = warm.shape[0]
    rx = lax.axis_index("rx")
    me = lax.axis_index("space")
    columns = peers // lines
    line = me // columns
    column = me % columns
    after = (rx, (me + 1) % peers)
    before = (rx, (me + peers - 1) % peers)
    others = []
    for k in range(0, rx_peers, 2):
        place = (rx + k) % rx_peers
        others += [(place, me)] * (k > 0) + [(place + 1 - 2 * (place % 2), me)]

    def at(line, column):
        return (rx, (line % lines) * columns + column % columns)

    along = [at(line, column + k) for k in range(1, columns)]
    across = [at(line + k, column) for k in range(1, lines)]
    rows_y = lines // 2
    half = (line // rows_y) * rows_y
    high_x = max(rx_peers // 2, 1)

    def beside(k):
        return at(half + (line + k + rows_y) % rows_y, column)

    def along_x(k):
        place = (2 * (rx // 2) + line // rows_y + k + 2 * high_x) % (2 * high_x)
        place_line = (place % 2) * rows_y + line % rows_y
        return (2 * (place // 2) + rx % 2, place_line * columns + column)

    opposite = at(line + rows_y, column)
    core = others[0]

    starts = [(s, p) for s in range(count) for p in range(2)]
    loads = [
        pltpu.make_async_copy(src, dst, load_sem.at[i])
        for i, (src, dst) in enumerate(
            [(warm_hbm.at[s, p], warm.at[s, p]) for s, p in starts]
            + [
                (cond_hbm, cond),
                (weight_hbm, weight),
                (cell_hbm, cell),
                (group_hbm, group),
                (freq_hbm, freq),
                (back_hbm, back),
            ]
        )
    ]
    for load in loads[: len(starts) + 1]:
        load.start()
    barrier = pltpu.get_barrier_semaphore()
    ring_z = [at(line, column + 1), at(line, column - 1)]
    ring_x = [along_x(1), along_x(-1)]
    ring_y = [beside(1), beside(-1)] if rows_y > 1 else []
    partners = [before, after, core] + ring_z + ring_x + ring_y
    for partner in partners:
        pl.semaphore_signal(barrier, inc=1, device_id=partner, device_id_type=MESH)
    for load in loads[len(starts) + 1 : -1]:
        load.start()

    meetings = [list(ring_x), [core], [opposite]]
    reach, k = 1, 0
    while reach < max(columns, rows_y) // 2:
        if k == len(meetings):
            meetings.append([])
        if reach < columns // 2:
            meetings[k] += [at(line, column + reach), at(line, column - reach)]
        if reach < rows_y // 2:
            meetings[k] += [beside(reach), beside(-reach)]
        reach, k = 2 * reach, k + 1
    taken = []

    def meet(steps):
        while len(taken) < min(steps, len(meetings) + 1):
            step = len(taken)
            if step > 0:
                pl.semaphore_wait(meet_sem.at[step - 1], len(meetings[step - 1]))
            if step < len(meetings):
                for target in meetings[step]:
                    pl.semaphore_signal(
                        meet_sem.at[step], inc=1, device_id=target, device_id_type=MESH
                    )
            taken.append(step)

    for load in loads[: len(starts) + 1]:
        load.wait()
    iy = lax.broadcasted_iota(jnp.int32, (height, breadth), 0)
    iz = lax.broadcasted_iota(jnp.int32, (height, breadth), 1)
    flat = iy * breadth + iz

    def y_up(f):
        return jnp.where(iy == height - 1, 0.0, pltpu.roll(f, height - 1, 0))

    def y_down(f):
        return jnp.where(iy == 0, 0.0, pltpu.roll(f, 1, 0))

    def z_up(f):
        return jnp.where(iz == breadth - 1, 0.0, pltpu.roll(f, breadth - 1, 1))

    def z_down(f):
        return jnp.where(iz == 0, 0.0, pltpu.roll(f, 1, 1))

    def outflow(k, i, first_plane, last_plane):
        ex, ey, ez = last_plane
        send[k, 0, 0, i] = (ey + (y_up(ex) - ex)).astype(jnp.bfloat16)
        send[k, 0, 1, i] = (ez + (z_up(ex) - ex)).astype(jnp.bfloat16)
        send[k, 1, 0, i] = first_plane[1].astype(jnp.bfloat16)
        send[k, 1, 1, i] = first_plane[2].astype(jnp.bfloat16)

    def pack(i, carry):
        s, p = i // 2, i % 2
        outflow(0, i, [warm[s, p, c, 0] for c in range(3)], [warm[s, p, c, last] for c in range(3)])
        return carry

    last = depth - 1
    lax.fori_loop(0, 2 * count, pack, 0, unroll=2)
    pl.semaphore_wait(barrier, len(partners))

    def halo(k, way, source, place):
        return pltpu.make_async_remote_copy(
            source,
            place,
            send_sem.at[way, k],
            recv_sem.at[way, k],
            device_id=(after, before)[way],
            device_id_type=MESH,
        )

    flows = [[halo(k, way, send.at[k, way], land.at[k, way]) for way in (0, 1)] for k in range(ITERS)]
    coefs = [halo(ITERS, 0, cond.at[last], cland.at[0]), halo(ITERS, 1, cond.at[0], cland.at[1])]
    for copy in flows[0] + coefs:
        copy.start()
    loads[-1].start()
    meet(1)

    for load in loads[len(starts) + 1 : -1]:
        load.wait()
    has_before = (me > 0).astype(jnp.float32)
    has_after = (me < peers - 1).astype(jnp.float32)
    def angular_of(s):
        k = freq[group[s]]
        low = jnp.where(k % 2 == 1, jnp.float32(1.25), jnp.float32(1.0))
        mid = jnp.where((k // 2) % 2 == 1, jnp.float32(1.25**2), jnp.float32(1.0))
        top = jnp.where((k // 4) % 2 == 1, jnp.float32(1.25**4), jnp.float32(1.0))
        return 0.25 * (low * mid * top)

    def angular_of(s):
        k = freq[group[s]]
        low = jnp.where(k % 2 == 1, jnp.float32(1.25), jnp.float32(1.0))
        mid = jnp.where((k // 2) % 2 == 1, jnp.float32(1.25**2), jnp.float32(1.0))
        top = jnp.where((k // 4) % 2 == 1, jnp.float32(1.25**4), jnp.float32(1.0))
        return 0.25 * (low * mid * top)

    def guard(plane, f):
        if plane < depth:
            return f * has_before
        if plane >= 2 * depth:
            return f * has_after
        return f

    def start_plane(s, p, c, plane):
        if plane < depth:
            return guard(plane, land[0, plane, c, 2 * s + p].astype(jnp.float32))
        if plane >= 2 * depth:
            return guard(plane, land[1, plane - 2 * depth, c, 2 * s + p].astype(jnp.float32))
        return warm[s, p, c, plane - depth]

    def cond_plane(plane):
        if plane < depth:
            return cland[0, plane].astype(jnp.float32)
        if plane >= 2 * depth:
            return cland[1, plane - 2 * depth].astype(jnp.float32)
        return cond[plane - depth]

    def inflow_low(first_part, second_part, weight_):
        return (0.0, weight_ * first_part, weight_ * second_part)

    def inflow_high(ey, ez, weight_):
        div = (ey - y_down(ey)) + (ez - z_down(ez))
        return (-weight_ * div, weight_ * ey, weight_ * ez)

    def step(s, p, old, other, coef, with_source):
        turn = (1 - 2 * p).astype(jnp.float32) * (RELAX * angular_of(s))
        planes = len(old)
        hy_low, hz_low = -old[0][2], old[0][1]
        new = []
        for plane in range(planes):
            ex, ey, ez = old[plane]
            hx = (y_up(ez) - ez) - (z_up(ey) - ey)
            hy = (z_up(ex) - ex) + ez
            hz = (ex - y_up(ex)) - ey
            if plane < planes - 1:
                hy = hy - old[plane + 1][2]
                hz = hz + old[plane + 1][1]
            curl = (
                (hz - y_down(hz)) - (hy - z_down(hy)),
                (hx - z_down(hx)) - (hz - hz_low),
                (hy - hy_low) - (hx - y_down(hx)),
            )
            hy_low, hz_low = hy, hz
            factor = turn * coef(plane)
            fresh = [old[plane][c] - RELAX * curl[c] + factor * other(c, plane) for c in range(3)]
            if with_source:
                point = flat == cell[s] - (me * depth + plane) * (height * breadth)
                fresh = [
                    fresh[c] + jnp.where(point, RELAX * weight[s, p, c], 0.0) for c in range(3)
                ]
            new.append(fresh)
        return new

    def from_warm(i, c, plane):
        return warm[i // 2, i % 2, c, plane]

    def held(buffer):
        return lambda i, c, plane: buffer[i, c, plane]

    def sweep(source, target, with_source, send_slot=None):
        def one(i, carry):
            s, p = i // 2, i % 2
            old = [[source(i, c, plane) for c in range(3)] for plane in range(depth)]
            twin = i + 1 - 2 * p
            new = step(
                s, p, old, lambda c, plane: source(twin, c, plane), lambda k: cond[k], with_source
            )
            for plane in range(depth):
                for c in range(3):
                    target[i, c, plane] = new[plane][c]
            if send_slot is not None:
                outflow(send_slot, i, new[0], new[last])
            return carry

        lax.fori_loop(0, 2 * count, one, 0, unroll=2)

    sweep(from_warm, alone_1, True, 1)
    for copy in flows[1]:
        copy.start()
    sweep(held(alone_1), alone_2, True, 2)
    for copy in flows[2]:
        copy.start()
    sweep(held(alone_2), alone_3, True)

    def answer(i, carry):
        first_plane = [from_warm(i, c, 0) for c in range(3)]
        ex, ey, ez = [from_warm(i, c, last) for c in range(3)]
        low = inflow_high(first_plane[1], first_plane[2], RELAX)
        high = inflow_low(ey + (y_up(ex) - ex), ez + (z_up(ex) - ex), RELAX)
        echo[0, i, 0], echo[0, i, 1], echo[0, i, 2] = low
        echo[1, i, 0], echo[1, i, 1], echo[1, i, 2] = jnp.zeros_like(ex), high[1], high[2]
        extra[0, 0, 0, i] = low[1] + (y_up(low[0]) - low[0])
        extra[0, 0, 1, i] = low[2] + (z_up(low[0]) - low[0])
        extra[0, 1, 0, i] = high[1]
        extra[0, 1, 1, i] = high[2]
        return carry

    lax.fori_loop(0, 2 * count, answer, 0, unroll=2)
    meet(2)
    for copy in coefs:
        copy.wait_recv()

    def answer_again(i, carry):
        s, p = i // 2, i % 2
        twin = i + 1 - 2 * p
        for way in range(2):
            new = step(
                s,
                p,
                [[echo[way, i, c] for c in range(3)]],
                lambda c, plane: echo[way, twin, c],
                lambda k: cland[way],
                False,
            )
            for c in range(3):
                reply[way, i, c] = new[0][c]
        return carry

    lax.fori_loop(0, 2 * count, answer_again, 0, unroll=2)

    weight_low, weight_high = RELAX * has_before, RELAX * has_after
    for copy in flows[0]:
        copy.wait_recv()

    def arrival_0(i, carry):
        got = [[land[0, way, j, i].astype(jnp.float32) for j in range(2)] for way in range(2)]
        low = inflow_low(got[0][0], got[0][1], weight_low)
        high = inflow_high(got[1][0], got[1][1], weight_high)
        zero = jnp.zeros((height, breadth), jnp.float32)
        for c in range(3):
            delta_1[i, c, 0] = low[c] + zero
            delta_1[i, c, last] = high[c]
            for plane in range(1, last):
                delta_1[i, c, plane] = zero
        near = [alone_1[i, c, 0] + low[c] for c in range(3)]
        ex, ey, ez = [alone_1[i, c, last] + high[c] for c in range(3)]
        low = inflow_high(near[1], near[2], RELAX)
        low = [reply[0, i, c] + low[c] for c in range(3)]
        high = inflow_low(ey + (y_up(ex) - ex), ez + (z_up(ex) - ex), RELAX)
        extra[1, 0, 0, i] = low[1] + (y_up(low[0]) - low[0])
        extra[1, 0, 1, i] = low[2] + (z_up(low[0]) - low[0])
        extra[1, 1, 0, i] = reply[1, i, 1] + high[1]
        extra[1, 1, 1, i] = reply[1, i, 2] + high[2]
        return carry

    lax.fori_loop(0, 2 * count, arrival_0, 0, unroll=2)
    sweep(held(delta_1), delta_2, False)

    def total_inflow(k, i):
        got = [
            [land[k, way, j, i].astype(jnp.float32) + extra[k - 1, way, j, i] for j in range(2)]
            for way in range(2)
        ]
        low = inflow_low(got[0][0], got[0][1], weight_low)
        return low, inflow_high(got[1][0], got[1][1], weight_high)

    for copy in flows[1]:
        copy.wait_recv()

    def arrival_1(i, carry):
        low, high = total_inflow(1, i)
        for c in range(3):
            if c > 0:
                delta_2[i, c, 0] = delta_2[i, c, 0] + low[c]
            delta_2[i, c, last] = delta_2[i, c, last] + high[c]
        return carry

    lax.fori_loop(0, 2 * count, arrival_1, 0, unroll=2)
    sweep(held(delta_2), delta_3, False)

    slots = [0, last] + list(range(1, last))

    def product(s, plane, real_part, imag_part):
        g = group[s]
        angular = angular_of(s)
        real = jnp.zeros((height, breadth), jnp.float32)
        imag = jnp.zeros((height, breadth), jnp.float32)
        for c in range(3):
            fr, fi = back[g, 0, c, plane], back[g, 1, c, plane]
            real += fr * real_part[c] - fi * imag_part[c]
            imag += fr * imag_part[c] + fi * real_part[c]
        coef = angular * cond[plane]
        rows[rx, slots.index(plane), 2 * s] = (coef * real).astype(jnp.bfloat16)
        rows[rx, slots.index(plane), 2 * s + 1] = (coef * imag).astype(jnp.bfloat16)

    def swept(i, plane):
        return [alone_3[i, c, plane] + delta_3[i, c, plane] for c in range(3)]

    def inner_products(s, carry):
        for plane in range(1, last):
            product(s, plane, swept(2 * s, plane), swept(2 * s + 1, plane))
        return carry

    loads[-1].wait()
    lax.fori_loop(0, count, inner_products, 0, unroll=2)

    def edge(part, way):
        plane = ((last - 1, 1), (last, 0))[part][way]
        place = ((0, 1), (1, 0))[part][way]
        return pltpu.make_async_remote_copy(
            rows.at[rx, slots.index(plane)],
            rland.at[way, place],
            rsend_sem.at[part, way],
            rrecv_sem.at[part, way],
            device_id=(after, before)[way],
            device_id_type=MESH,
        )

    def to_group(part, k):
        span = (pl.ds(2, depth - 2), pl.ds(0, 2))[part]
        slot = (rx, rx, (rx + 2) % rx_peers)[k]
        return pltpu.make_async_remote_copy(
            rows.at[slot, span],
            rows.at[slot, span],
            gsend_sem.at[part, k],
            grecv_sem.at[part, k],
            device_id=others[(0, 1, 0)[k]],
            device_id_type=MESH,
        )

    edges = [edge(part, way) for part in range(2) for way in range(2)]
    gather = [[to_group(part, k) for k in range(rx_peers - 1)] for part in range(2)]
    meet(3)
    for copy in gather[0][:2] + edges[:2]:
        copy.start()
    for copy in flows[2]:
        copy.wait_recv()

    def outer_products(s, carry):
        parts = []
        for i in (2 * s, 2 * s + 1):
            low, high = total_inflow(2, i)
            near, far = swept(i, 0), swept(i, last)
            parts.append(
                ([near[c] + low[c] for c in range(3)], [far[c] + high[c] for c in range(3)])
            )
        product(s, 0, parts[0][0], parts[1][0])
        product(s, last, parts[0][1], parts[1][1])
        return carry

    lax.fori_loop(0, count, outer_products, 0, unroll=2)
    for copy in gather[1][:2] + edges[2:]:
        copy.start()
    def within(f):
        return f + KAPPA * (y_up(f) + y_down(f) + z_up(f) + z_down(f) - 6.0 * f)

    def smooth_own(r, carry):
        own = [rows[rx, slots.index(k), r].astype(jnp.float32) for k in range(depth)]
        once = [within(f) for f in own]
        for k in range(depth):
            if k > 0:
                once[k] += KAPPA * own[k - 1]
            if k < last:
                once[k] += KAPPA * own[k + 1]
        once = [(KAPPA * has_before) * own[0]] + once + [(KAPPA * has_after) * own[last]]
        for k in range(depth):
            twice[r, k] = within(once[k + 1]) + KAPPA * (once[k] + once[k + 2])
        return carry

    lax.fori_loop(0, 2 * count, smooth_own, 0, unroll=2)
    if rx_peers > 2:
        for part in range(2):
            gather[part][1].wait_recv()
            gather[part][2].start()
    for copy in edges:
        copy.wait_recv()

    def smooth_edges(r, carry):
        value = [twice[r, k] for k in range(depth)]
        for has, ends, border, inner in (
            (has_before, (0, 1), 0, 1),
            (has_after, (1, 0), last, last - 1),
        ):
            way = 0 if border == 0 else 1
            far, near = (rland[way, k, r].astype(jnp.float32) * has for k in ends)
            value[border] += (2.0 * KAPPA) * within(near) + (KAPPA * KAPPA) * far
            value[inner] += (KAPPA * KAPPA) * near
        for k in range(depth):
            rounded = value[k].astype(jnp.bfloat16)
            smooth[r, k] = rounded
            twice[r, k] = rounded.astype(jnp.float32)
        return carry

    lax.fori_loop(0, 2 * count, smooth_edges, 0, unroll=2)

    for part in range(2):
        gather[part][0].wait_recv()
    wide = 2 * count * rx_peers

    def dots(b, carry):
        peer, r = (rx - rx % 2 + b // (2 * count)) % rx_peers, b % (2 * count)
        right = [rows[peer, slots.index(k), r].astype(jnp.float32) for k in range(depth)]
        for a in range(2 * count):
            total = jnp.zeros((8, breadth), jnp.float32)
            for k in range(depth):
                product = twice[a, k] * right[k]
                for j in range(height // 8):
                    total += product[8 * j : 8 * j + 8]
            sums[a, peer * (2 * count) + r] = jnp.sum(total, axis=0)
        return carry

    lax.fori_loop(0, 4 * count, dots, 0, unroll=2)
    if rx_peers > 2:
        for part in range(2):
            gather[part][2].wait_recv()
    lax.fori_loop(4 * count, wide, dots, 0, unroll=2)
    ones = jnp.ones((8, breadth), jnp.bfloat16)
    by_lane = sums[...].reshape(2 * count * wide, breadth)
    high = by_lane.astype(jnp.bfloat16)
    low = (by_lane - high.astype(jnp.float32)).astype(jnp.bfloat16)
    lanes = [
        lax.dot_general(
            ones, part, (((1,), (1,)), ((), ())), preferred_element_type=jnp.float32
        )
        for part in (high, low)
    ]
    line_sums[column] = jnp.zeros(line_sums.shape[1:], jnp.float32)
    line_sums[column, :, 0 : 2 * count * wide] = (lanes[0] + lanes[1])[0:1]

    step_one = [
        pltpu.make_async_remote_copy(
            line_sums.at[column],
            line_sums.at[column],
            ssend_sem.at[0, k],
            srecv_sem.at[0, k],
            device_id=target,
            device_id_type=MESH,
        )
        for k, target in enumerate(along)
    ]
    meet(len(meetings) + 1)
    for copy in step_one:
        copy.start()
    for copy in step_one:
        copy.wait_recv()
    plane_sums[line] = jnp.sum(line_sums[...], axis=0)
    step_two = [
        pltpu.make_async_remote_copy(
            plane_sums.at[line],
            plane_sums.at[line],
            ssend_sem.at[1, k],
            srecv_sem.at[1, k],
            device_id=target,
            device_id_type=MESH,
        )
        for k, target in enumerate(across)
    ]
    for copy in step_two:
        copy.start()
    for copy in step_two:
        copy.wait_recv()
    total = jnp.sum(plane_sums[...], axis=0)
    cells = depth * height * breadth * peers
    for a in range(2 * count):
        block_ref[a : a + 1, :] = total[:, a * wide : (a + 1) * wide] / cells
    for copy in sum(flows, []) + coefs + edges + gather[0] + gather[1] + step_one + step_two:
        copy.wait_send()


def deliver(block, smooth, block_out, smooth_out, sem):
    copies = [
        pltpu.make_async_copy(smooth, smooth_out, sem.at[0]),
        pltpu.make_async_copy(block, block_out, sem.at[1]),
    ]
    for copy in copies:
        copy.start()
    for copy in copies:
        copy.wait()


def shards(conductivity, background, warm_start, data_weight, recv_cell, src_group, group_freq):
    count = warm_start.shape[0]
    depth, height, breadth = conductivity.shape
    peers, rx_peers = lax.axis_size("space"), lax.axis_size("rx")
    lines = 1
    while lines * lines < peers:
        lines *= 2
    columns = peers // lines
    rows = 2 * count
    wide = rows * rx_peers
    plane = (height, breadth)
    f32, b16 = jnp.float32, jnp.bfloat16
    vmem, dma = pltpu.VMEM, pltpu.SemaphoreType.DMA
    hbm = pl.BlockSpec(memory_space=pltpu.HBM)
    operands = (
        conductivity,
        background,
        warm_start,
        data_weight,
        recv_cell,
        src_group,
        group_freq,
    )
    pinned = [pltpu.with_memory_space_constraint(x, pltpu.HBM) for x in operands]
    block, smoothed = pl.pallas_call(
        functools.partial(kernel, peers, lines, rx_peers),
        name="inversion_step",
        out_shape=(
            pltpu.VMEM((rows, wide), f32),
            pltpu.VMEM((rows, depth) + plane, b16),
        ),
        in_specs=[hbm] * 7,
        out_specs=(pl.BlockSpec(memory_space=vmem), pl.BlockSpec(memory_space=vmem)),
        scratch_shapes=[
            vmem(conductivity.shape, f32),
            vmem(background.shape, f32),
            vmem(warm_start.shape, f32),
            pltpu.SMEM(data_weight.shape, f32),
            pltpu.SMEM(recv_cell.shape, jnp.int32),
            pltpu.SMEM(src_group.shape, jnp.int32),
            pltpu.SMEM(group_freq.shape, jnp.int32),
            vmem((ITERS, 2, 2, rows) + plane, b16),
            vmem((ITERS, 2, 2, rows) + plane, b16),
            vmem((2,) + plane, f32),
        ]
        + [vmem((rows, 3, depth) + plane, f32)] * 6
        + [vmem((2, rows, 3) + plane, f32)] * 2
        + [
            vmem((ITERS - 1, 2, 2, rows) + plane, f32),
            vmem((rx_peers, depth, rows) + plane, b16),
            vmem((2, 2, rows) + plane, b16),
            vmem((rows, depth) + plane, f32),
            vmem((rows, wide, breadth), f32),
            vmem((columns, 1, breadth), f32),
            vmem((lines, 1, breadth), f32),
            dma((rows + 6,)),
            dma((2, ITERS + 1)),
            dma((2, ITERS + 1)),
            dma((2, 2)),
            dma((2, 2)),
            dma((2, rx_peers - 1)),
            dma((2, rx_peers - 1)),
            dma((2, max(lines, columns) - 1)),
            dma((2, max(lines, columns) - 1)),
            pltpu.SemaphoreType.REGULAR((3,)),
        ],
        compiler_params=pltpu.CompilerParams(
            collective_id=0, has_side_effects=True, vmem_limit_bytes=48 * 2**20
        ),
    )(*pinned)
    results = [pltpu.with_memory_space_constraint(x, vmem) for x in (block, smoothed)]
    block, smoothed = pl.pallas_call(
        deliver,
        name="deliver",
        out_shape=(pltpu.HBM((rows, wide), f32), pltpu.HBM((rows, depth) + plane, b16)),
        in_specs=[pl.BlockSpec(memory_space=vmem)] * 2,
        out_specs=(hbm, hbm),
        scratch_shapes=[dma((2,))],
    )(*results)
    return block, smoothed.reshape((count, 2, depth) + plane)


def solution(mesh):
    in_specs = (
        P("space", None, None),
        P(None, None, None, "space", None, None),
        P("rx", None, None, "space", None, None),
        P("rx", None, None),
        P("rx"),
        P("rx"),
        P(),
    )
    out_specs = (P("rx", None), P("rx", None, "space", None, None))
    return jax.shard_map(shards, mesh=mesh, in_specs=in_specs, out_specs=out_specs, check_vma=False)
```
